256 devices in a mesh: ctx: 64 (over y, x_hi, z), head: 4 (over x_lo, core).
Axes of the slice: x: 4 (x_hi: 2, x_lo: 2; x = x_hi * 2 + x_lo), y: 4, z: 8, core: 2. Of those that a mesh axis runs over, the one named last changes fastest.
Arguments:
- queries: bfloat16 [1024, 64, 128], P('ctx', 'head'), may hold values from -12 to 12
- cache_keys: bfloat16 [65536, 4, 128], P('ctx', 'head'), may hold values from -6 to 6
- cache_values: bfloat16 [65536, 4, 128], P('ctx', 'head'), may hold values from -24 to 24
- new_keys: bfloat16 [1024, 4, 128], P('ctx', 'head'), may hold values from -6 to 6
- new_values: bfloat16 [1024, 4, 128], P('ctx', 'head'), may hold values from -24 to 24
- block_chat: int32 [512], P('ctx'), may hold values from 0 to 3, as said below
- block_fill: int32 [512], P('ctx'), may hold values from 1 to 128, as said below
- new_chat: int32 [1024], P('ctx'), may hold values from 0 to 3, never falling along the last dimension, each value on 1 to 512 neighbouring positions
Outputs:
- attended: bfloat16 [1024, 8192], P(('ctx', 'head'))
The draws below stay inside these ranges and needn't reach their ends.
Inputs may be any that keep to these rules, and one draw needn't show every extreme that they name: `block_chat`: each of the 4 chats owns one or more whole blocks of 128 rows; the blocks listed chat by chat are dealt to the devices of ctx in turn, one slot after another. `block_fill`: every block is full except the last block of each chat. `new_chat`: chats follow one another in order, each one or more tokens.
All inputs are finite; a program needn't handle non-finite values.
Results may differ from the reference program's by a relative error of at most 0.0065.
Values may be sent and summed in bfloat16 or wider, within the bound.
No kernel may reach another device: no remote copies, remote signals or barrier semaphores. Data moves between devices by JAX's collectives and lax.ppermute only.
A program may use at most 128 MiB of HBM per device.

```python
import math
import jax
import jax.numpy as jnp
import numpy as np
from jax import lax

HD = 128
GROUP = 16
CHATS = 4
BLOCK = 128
CACHE_DEV = 1024
KV_HEADS = 4
QH = 64
CACHE = 65536
NEW = 1024


def block_layout(key):
    key_cut, key_fill = jax.random.split(jax.random.fold_in(key, 17))
    count = CACHE // BLOCK
    per_device = CACHE_DEV // BLOCK
    devices = count // per_device
    cuts = jnp.sort(jax.random.permutation(key_cut, count - 1)[:CHATS - 1] + 1)
    storage = jnp.arange(count)
    listed = storage % per_device * devices + storage // per_device
    chats = jnp.sum(listed[:, None] >= cuts[None, :], axis=1).astype(jnp.int32)
    ends = jnp.concatenate([cuts - 1, jnp.array([count - 1])])
    last_one = jnp.any(listed[:, None] == ends[None, :], axis=1)
    partial_fill = jax.random.randint(key_fill, (count,), 1, BLOCK + 1)
    fills = jnp.where(last_one, partial_fill, BLOCK).astype(jnp.int32)
    return (chats, fills)


def draw_block_chat(key, part):
    return block_layout(key)[0]


def draw_block_fill(key, part):
    return block_layout(key)[1]


def draw_queries(key, part):
    key = jax.random.fold_in(key, 3)
    base = jnp.clip(2.0 * jax.random.normal(key, (NEW, QH, HD), jnp.float32), -12.0, 12.0)
    return base.astype(jnp.bfloat16)


def draw_new_keys(key, part):
    key = jax.random.fold_in(key, 5)
    base = jnp.clip(jax.random.normal(key, (NEW, KV_HEADS, HD), jnp.float32), -6.0, 6.0)
    return base.astype(jnp.bfloat16)


def block_levels(key, dims, shards, least, high):
    level = 1.0
    for dim, blocks in shards:
        steps = jax.random.uniform(jax.random.fold_in(jax.random.fold_in(key, 6), dim), (blocks,), jnp.float32, least / len(shards), high / len(shards))
        level = level * jnp.repeat(jnp.exp(steps), dims[dim] // blocks).reshape((-1,) + (1,) * (len(dims) - 1 - dim))
    return level


def split_up(amount, total, bound, lean):
    loads = [(1 << 20) // math.isqrt(standing ** lean) + 1 for standing in range(2, amount + 1)]
    surplus, holding = total - bound - (amount - 1), [1] * (amount - 1)
    while surplus > 0:
        movable = [i for i in range(amount - 1) if holding[i] < bound]
        mass, remaining = sum([loads[i] for i in movable]), surplus
        for i in movable:
            addition = min(bound - holding[i], max(1, remaining * loads[i] // mass), surplus)
            holding[i] = holding[i] + addition
            surplus = surplus - addition
    return np.array([bound] + holding)


def ragged_sizes(key, amount, total, most, skew):
    if amount == 2:
        one = jax.random.randint(key, (), max(1, total - most), min(most, total - 1) + 1)
        return jnp.stack([one, total - one])
    sizes = jnp.asarray(split_up(amount, total, most, skew), jnp.int32)
    couples = (amount - 1) // 2
    giver, receiver = sizes[1:1 + 2 * couples:2], sizes[2:2 + 2 * couples:2]
    margin = jnp.minimum(giver - 1, most - receiver)
    moved = jax.random.randint(jax.random.fold_in(key, 1), (couples,), 0, 1 << 20) % (margin + 1)
    sizes = sizes.at[1:1 + 2 * couples:2].set(giver - moved).at[2:2 + 2 * couples:2].set(receiver + moved)
    return sizes[jax.random.permutation(jax.random.fold_in(key, 2), amount)]


def gaussian(own_key, shape, width, bound, cuts=(), held_as=jnp.bfloat16):
    entries = jax.random.normal(own_key, shape, jnp.float32) * width
    if len(cuts) > 0:
        entries = block_levels(own_key, shape, cuts, -0.22, 0.18) * entries
    return jnp.clip(entries, min=-bound, max=bound).astype(held_as)


def setup_inputs(seed: int = 0) -> dict:
    key_of = jax.random.split(jax.random.key(seed), 9)
    queries = draw_queries(jax.random.fold_in(key_of[8], 71), 0)
    cache_keys = gaussian(key_of[1], (CACHE, KV_HEADS, HD), 1.0, 6.0, ((0, 64), (1, 4)))
    cache_values = gaussian(key_of[2], (CACHE, KV_HEADS, HD), 4.0, 24.0, ((0, 64), (1, 4)))
    new_keys = draw_new_keys(jax.random.fold_in(key_of[8], 71), 0)
    new_values = gaussian(key_of[4], (NEW, KV_HEADS, HD), 4.0, 24.0, ((0, 64), (1, 4)))
    block_chat = draw_block_chat(jax.random.fold_in(key_of[8], 71), 0)
    block_fill = draw_block_fill(jax.random.fold_in(key_of[8], 71), 0)
    new_chat = jnp.searchsorted(jnp.cumsum(ragged_sizes(key_of[7], CHATS, NEW, NEW // 2, 2)), jnp.arange(NEW), side="right").astype(jnp.int32)
    return dict(queries=queries, cache_keys=cache_keys, cache_values=cache_values, new_keys=new_keys, new_values=new_values, block_chat=block_chat, block_fill=block_fill, new_chat=new_chat)


def reference(queries, cache_keys, cache_values, new_keys, new_values, block_chat, block_fill, new_chat):
    scale = HD ** -0.5
    within = jnp.arange(CACHE, dtype=jnp.int32) % BLOCK
    row_chat = jnp.repeat(block_chat.astype(jnp.int32), BLOCK)
    row_fill = jnp.repeat(block_fill.astype(jnp.int32), BLOCK)
    cache_chat = jnp.where(within < row_fill, row_chat, -1).astype(jnp.int32)
    key_chat = jnp.concatenate([cache_chat, new_chat.astype(jnp.int32)])
    key_pos = jnp.concatenate([jnp.full((CACHE,), -1, jnp.int32), jnp.arange(NEW, dtype=jnp.int32)])
    all_keys = jnp.concatenate([cache_keys, new_keys], 0).transpose(1, 0, 2)
    all_values = jnp.concatenate([cache_values, new_values], 0).transpose(1, 0, 2)
    grouped = queries.reshape(NEW, KV_HEADS, GROUP, HD).transpose(1, 0, 2, 3)
    span = 32
    batches = NEW // span
    query_chat = new_chat.astype(jnp.int32).reshape(batches, span)
    query_pos = jnp.arange(NEW, dtype=jnp.int32).reshape(batches, span)

    def one_head(operands):
        head_queries, head_keys, head_values = operands
        keys_wide = head_keys.astype(jnp.float32)
        values_wide = head_values.astype(jnp.float32)

        def one_batch(batch):
            batch_queries, batch_chat, batch_pos = batch
            scores = jnp.einsum('rgd,kd->rgk', batch_queries.astype(jnp.float32), keys_wide) * scale
            mask = (key_chat[None, :] == batch_chat[:, None]) & (key_pos[None, :] <= batch_pos[:, None])
            scores = jnp.where(mask[:, None, :], scores, -jnp.inf)
            largest = jnp.max(scores, axis=-1, keepdims=True)
            weights = jnp.where(mask[:, None, :], jnp.exp(scores - largest), 0.0)
            total = jnp.sum(weights, axis=-1)
            rounded = lax.optimization_barrier(weights.astype(jnp.bfloat16)).astype(jnp.float32)
            numerator = jnp.einsum('rgk,kd->rgd', rounded, values_wide)
            return (numerator / total[..., None]).astype(jnp.bfloat16)

        return lax.map(one_batch, (head_queries.reshape(batches, span, GROUP, HD), query_chat, query_pos))

    result = lax.map(one_head, (grouped, all_keys, all_values))
    return result.reshape(KV_HEADS, NEW, GROUP, HD).transpose(1, 0, 2, 3).reshape(NEW, QH * HD)
```

```python
import functools
import math

import jax
import jax.numpy as jnp
from jax import lax
from jax.experimental import pallas as pl
from jax.experimental.pallas import tpu as pltpu
from jax.sharding import Mesh, PartitionSpec as P

BLOCK = 128
SLOTS = 8
ROWS = SLOTS * BLOCK
TOK = 16
GROUP = 16
HD = 128
QR = TOK * GROUP
HALF = ROWS // 2
FRESH = 2 * TOK
MEMBERS = 8
FAR = -1e30
SCALE = HD**-0.5 * math.log2(math.e)
VMEM = pl.BlockSpec(memory_space=pltpu.VMEM)
SMEM = pl.BlockSpec(memory_space=pltpu.SMEM)
ANY = pl.BlockSpec(memory_space=pl.ANY)
CHAT, FILL, TOKEN_CHAT, START, DESC = 0, 8, 16, 32, 128


def params(limit=48 * 1024 * 1024):
    return pltpu.CompilerParams(vmem_limit_bytes=limit)


def prepare_kernel(place, bc, bf, nc, k, v, nk, nv, a, b, c, d, desc, sems):
    copies = [
        (k.at[pl.ds(0, HALF)], a.at[pl.ds(0, HALF)]),
        (nk, a.at[pl.ds(HALF, TOK)]),
        (nv, a.at[pl.ds(HALF + TOK, TOK)]),
        (k.at[pl.ds(HALF, HALF)], b),
        (v.at[pl.ds(0, HALF)], c),
        (v.at[pl.ds(HALF, HALF)], d),
    ]
    started = []
    for i, (src, dst) in enumerate(copies):
        copy = pltpu.make_async_copy(src, dst, sems.at[i])
        copy.start()
        started.append(copy)
    for i in range(SLOTS):
        desc[CHAT + i] = bc[i]
        desc[FILL + i] = bf[i]
    for i in range(TOK):
        desc[TOKEN_CHAT + i] = nc[i]
    desc[START] = place[0] * TOK
    for i in range(START + 1, DESC):
        desc[i] = 0
    for copy in started:
        copy.wait()


def prepare(place, bc, bf, nc, k, v, nk, nv):
    half = jax.ShapeDtypeStruct((HALF, HD), jnp.bfloat16)
    return pl.pallas_call(
        prepare_kernel,
        out_shape=[
            jax.ShapeDtypeStruct((HALF + FRESH, HD), jnp.bfloat16),
            half,
            half,
            half,
            jax.ShapeDtypeStruct((DESC,), jnp.int32),
        ],
        in_specs=[SMEM] * 4 + [ANY] * 4,
        out_specs=[ANY] * 4 + [SMEM],
        scratch_shapes=[pltpu.SemaphoreType.DMA((6,))],
        compiler_params=params(),
        name="prepare",
    )(place, bc, bf, nc, k, v, nk, nv)


def set_queries(q_refs, q_desc, qa):
    lane = lax.broadcasted_iota(jnp.int32, (TOK, HD), 1)
    for i in range(MEMBERS):
        qa[i * QR : (i + 1) * QR, 0:HD] = q_refs[i][...]
        for t in range(TOK):
            rows = slice(i * QR + t * GROUP, i * QR + (t + 1) * GROUP)
            hot = jnp.where(lane == q_desc[i][TOKEN_CHAT + t], 1.0, 0.0)
            qa[rows, HD : 2 * HD] = hot.astype(jnp.bfloat16)


def set_source(parts, desc, ka, va):
    a, b, c, d = parts
    ka[0:HALF, 0:HD] = a[0:HALF, :]
    ka[HALF:ROWS, 0:HD] = b[...]
    va[0:HALF, 0:HD] = c[...]
    va[HALF:ROWS, 0:HD] = d[...]
    va[:, HD : 2 * HD] = jnp.ones((ROWS, HD), jnp.bfloat16)
    lane = lax.broadcasted_iota(jnp.int32, (BLOCK, HD), 1)
    row = lax.broadcasted_iota(jnp.int32, (BLOCK, HD), 0)
    for s in range(SLOTS):
        live = (lane == desc[CHAT + s]) & (row < desc[FILL + s])
        ka[s * BLOCK : (s + 1) * BLOCK, HD : 2 * HD] = jnp.where(live, 0.0, FAR).astype(jnp.bfloat16)


def fold(state_in, state_out, rows, pieces):
    acc_in, ml_in = state_in
    acc_out, ml_out = state_out
    top = None
    for scores, _ in pieces:
        for j in range(scores.shape[1] // HD):
            tile = scores[:, j * HD : (j + 1) * HD]
            top = tile if top is None else jnp.maximum(top, tile)
    top = jnp.max(top, axis=1, keepdims=True)
    if acc_in is not None:
        ml = ml_in[rows, :]
        old, total = ml[:, 0:1], ml[:, HD // 2 : HD // 2 + 1]
        new = jnp.maximum(old, top)
    else:
        new = top
    summed = None
    for scores, values in pieces:
        weights = jnp.exp2((scores - new) * SCALE).astype(jnp.bfloat16)
        product = jnp.dot(weights, values, preferred_element_type=jnp.float32)
        summed = product if summed is None else summed + product
    acc, total_now = summed[:, 0:HD], summed[:, HD : 2 * HD]
    if acc_in is not None:
        factor = jnp.exp2((old - new) * SCALE)
        acc = acc + acc_in[rows, :] * factor
        total_now = total_now + total * factor
    lane = lax.broadcasted_iota(jnp.int32, (QR, HD), 1)
    acc_out[rows, :] = acc
    ml_out[rows, :] = jnp.where(lane < HD // 2, new, total_now)


def scores_of(q, keys):
    return lax.dot_general(q, keys, (((1,), (1,)), ((), ())), preferred_element_type=jnp.float32)


def attend_kernel(sources, first, last, *refs):
    refs = list(refs)
    take = lambda n: [refs.pop(0) for _ in range(n)]
    q_desc = take(MEMBERS)
    s_desc = take(MEMBERS if last else sources)
    q_refs = take(MEMBERS)
    parts = [take(4) for _ in range(sources)]
    fresh = take(MEMBERS) if last else []
    state_in = (None, None) if first else tuple(take(2))
    if last:
        outs, lses = take(MEMBERS), take(MEMBERS)
    else:
        state_out = tuple(take(2))
    qa = take(1)[0]
    ka, va = take(sources), take(sources)
    if last:
        na, nva = take(2)
        state_out = tuple(take(2))

    set_queries(q_refs, q_desc, qa)
    for s in range(sources):
        set_source(parts[s], s_desc[s], ka[s], va[s])
    if last:
        lane = lax.broadcasted_iota(jnp.int32, (TOK, HD), 1)
        row = lax.broadcasted_iota(jnp.int32, (TOK, HD), 0)
        key_lane = lax.broadcasted_iota(jnp.int32, (1, HD), 1)
        key_pos = jnp.zeros((1, HD), jnp.int32)
        for i in range(MEMBERS):
            at = slice(i * TOK, (i + 1) * TOK)
            na[at, 0:HD] = fresh[i][0:TOK, :]
            nva[at, 0:HD] = fresh[i][TOK : 2 * TOK, :]
            chat = jnp.zeros((TOK, HD), jnp.int32)
            for t in range(TOK):
                chat = jnp.where(row == t, s_desc[i][TOKEN_CHAT + t], chat)
            na[at, HD : 2 * HD] = jnp.where(lane == chat, 0.0, FAR).astype(jnp.bfloat16)
            key_pos = jnp.where(key_lane // TOK == i, s_desc[i][START] + key_lane % TOK, key_pos)
        nva[:, HD : 2 * HD] = jnp.ones((BLOCK, HD), jnp.bfloat16)
        token = lax.broadcasted_iota(jnp.int32, (QR, HD), 0) // GROUP

    for s in range(sources):
        source_in = state_in if s == 0 else state_out
        for c in range(MEMBERS):
            rows = slice(c * QR, (c + 1) * QR)
            low, high = q_desc[c][TOKEN_CHAT], q_desc[c][TOKEN_CHAT + TOK - 1]
            begin, end = jnp.int32(0), jnp.int32(0)
            for slot in range(SLOTS):
                chat = s_desc[s][CHAT + slot]
                begin += (chat < low).astype(jnp.int32)
                end += (chat <= high).astype(jnp.int32)
            count = end - begin

            def step(slots, rows=rows, c=c, s=s, begin=begin, source_in=source_in):
                at = pl.multiple_of(jnp.minimum(begin, SLOTS - slots) * BLOCK, BLOCK)
                keys, values = ka[s][pl.ds(at, slots * BLOCK), :], va[s][pl.ds(at, slots * BLOCK), :]
                q = qa[rows, :]
                pieces = [(scores_of(q, keys), values)]
                if last:
                    seen = key_pos <= q_desc[c][START] + token
                    fresh_scores = jnp.where(seen, scores_of(q, na[...]), FAR)
                    pieces.append((fresh_scores, nva[...]))
                fold(source_in, state_out, rows, pieces)

            pl.when(count <= 2)(functools.partial(step, 2))
            pl.when((count > 2) & (count <= 4))(functools.partial(step, 4))
            pl.when(count > 4)(functools.partial(step, SLOTS))

    if last:
        acc, ml = state_out
        for c in range(MEMBERS):
            rows = slice(c * QR, (c + 1) * QR)
            stats = ml[rows, :]
            total = stats[:, HD // 2 : HD // 2 + 1]
            outs[c][...] = (acc[rows, :] / total).astype(jnp.bfloat16)
            lse = stats[:, 0:1] * SCALE + jnp.log2(total)
            lses[c][...] = jnp.broadcast_to(lse, (QR, HD)).T[0:1, :]


def attend(q_desc, s_desc, queries, parts, fresh, state, last):
    sources, first = len(parts), state is None
    operands = [*q_desc, *s_desc, *queries, *[x for p in parts for x in p], *fresh]
    specs = [SMEM] * (len(q_desc) + len(s_desc)) + [VMEM] * (len(queries) + 4 * sources)
    specs += [pl.BlockSpec((FRESH, HD), lambda i: (HALF // FRESH, 0))] * len(fresh)
    if not first:
        operands += state
        specs += [VMEM, VMEM]
    rows = MEMBERS * QR
    state_shapes = [(rows, HD), (rows, HD)]
    if last:
        out_shape = [jax.ShapeDtypeStruct((QR, HD), jnp.bfloat16)] * MEMBERS
        out_shape += [jax.ShapeDtypeStruct((1, QR), jnp.float32)] * MEMBERS
    else:
        out_shape = [jax.ShapeDtypeStruct(s, jnp.float32) for s in state_shapes]
    scratch = [pltpu.VMEM((rows, 2 * HD), jnp.bfloat16)]
    scratch += [pltpu.VMEM((ROWS, 2 * HD), jnp.bfloat16)] * (2 * sources)
    if last:
        scratch += [pltpu.VMEM((BLOCK, 2 * HD), jnp.bfloat16)] * 2
        scratch += [pltpu.VMEM(s, jnp.float32) for s in state_shapes]
    return pl.pallas_call(
        functools.partial(attend_kernel, sources, first, last),
        grid=(1,),
        out_shape=out_shape,
        in_specs=specs,
        out_specs=[VMEM] * len(out_shape),
        scratch_shapes=scratch,
        compiler_params=params(),
        cost_estimate=pl.CostEstimate(
            flops=sources * 4 * rows * ROWS * HD,
            bytes_accessed=sources * ROWS * HD * 4 + rows * HD * 18,
            transcendentals=sources * rows * ROWS,
        ),
        name="attend_last" if last else "attend",
    )(*operands)


def merge_kernel(place, *refs):
    parts, lses, outs, held = refs[:MEMBERS], refs[MEMBERS : 2 * MEMBERS], refs[2 * MEMBERS : -1], refs[-1]
    top = lses[0][...]
    for lse in lses[1:]:
        top = jnp.maximum(top, lse[...])
    shares = [jnp.exp2(lse[...] - top) for lse in lses]
    whole = shares[0]
    for share in shares[1:]:
        whole = whole + share
    total = None
    for part, share in zip(parts, shares):
        column = jnp.broadcast_to(share / whole, (HD, QR)).T
        term = part[...].astype(jnp.float32) * column
        total = term if total is None else total + term
    held[...] = total
    for i, out in enumerate(outs):
        at = pl.multiple_of(jnp.bitwise_xor(place[1], i) * (QR // 4), QR // 4)
        out[...] = held[pl.ds(at, QR // 4), :].astype(jnp.bfloat16)


def merge(place, parts, lses):
    return pl.pallas_call(
        merge_kernel,
        out_shape=[jax.ShapeDtypeStruct((QR // 4, HD), jnp.bfloat16)] * 4,
        in_specs=[SMEM] + [VMEM] * (2 * MEMBERS),
        out_specs=[VMEM] * 4,
        scratch_shapes=[pltpu.VMEM((QR, HD), jnp.float32)],
        compiler_params=params(),
        name="merge",
    )(place, *parts, *lses)


def lay_kernel(place, *refs):
    pieces, out, held = refs[:4], refs[4], refs[5]
    for i, piece in enumerate(pieces):
        held[...] = piece[...].astype(jnp.float32)
        first = jnp.bitwise_xor(place[1], i) * GROUP
        for h in range(GROUP):
            at = pl.multiple_of((first + h) * HD, HD)
            out[:, pl.ds(at, HD)] = held[pl.ds(h, TOK // 4, stride=GROUP), :].astype(jnp.bfloat16)


def lay(place, pieces):
    return pl.pallas_call(
        lay_kernel,
        out_shape=jax.ShapeDtypeStruct((TOK // 4, 4 * GROUP * HD), jnp.bfloat16),
        in_specs=[SMEM] + [VMEM] * 4,
        out_specs=VMEM,
        scratch_shapes=[pltpu.VMEM((QR // 4, HD), jnp.float32)],
        compiler_params=params(),
        name="lay",
    )(place, *pieces)


YX = ("y", "xh")
HEAD = ("xl", "core")
STEPS = [(dy, dx) for dy in range(4) for dx in range(2)]


def to_group(x, step, sign=1):
    dy, dx = step
    pairs = [
        (y * 2 + h, ((y + sign * dy) % 4) * 2 + (h + dx) % 2) for y in range(4) for h in range(2)
    ]
    return lax.ppermute(x, YX, pairs)


def along(x, step):
    return lax.ppermute(x, "z", [(i, (i + step) % MEMBERS) for i in range(MEMBERS)])


def per_device(queries, cache_keys, cache_values, new_keys, new_values, block_chat, block_fill, new_chat):
    ctx = lax.axis_index(("y", "xh", "z"))
    place = jnp.stack([ctx, lax.axis_index(HEAD)]).astype(jnp.int32)
    q = queries.reshape(QR, HD)
    a, b, c, d, desc = prepare(
        place,
        block_chat,
        block_fill,
        new_chat,
        cache_keys[:, 0, :],
        cache_values[:, 0, :],
        new_keys[:, 0, :],
        new_values[:, 0, :],
    )
    mine = (a, b, c, d, desc)
    qs = [q] + [to_group(q, s) for s in STEPS[1:]]
    q_desc = [desc] + [to_group(desc, s) for s in STEPS[1:]]

    def call(blocks, state):
        return attend(q_desc, [x[4] for x in blocks], qs, [x[:4] for x in blocks], [], state, False)

    state = None
    up = down = mine
    waiting, met = [mine], [mine]
    for _ in range(3):
        up, down = [along(x, 1) for x in up], [along(x, -1) for x in down]
        state = call(waiting, state)
        waiting = [up, down]
        met += waiting
    far = [along(up[0], 1), along(up[1], 1), along(down[2], -1), along(down[3], -1), along(up[4], 1)]
    state = call(waiting, state)
    met = [far] + met
    outs = attend(q_desc, [x[4] for x in met], qs, [far[:4]], [x[0] for x in met], state, True)
    parts, lses = list(outs[:MEMBERS]), list(outs[MEMBERS:])
    parts = [parts[0]] + [to_group(x, s, -1) for x, s in zip(parts[1:], STEPS[1:])]
    lses = [lses[0]] + [to_group(x, s, -1) for x, s in zip(lses[1:], STEPS[1:])]
    pieces = merge(place, parts, lses)
    pieces = [pieces[0]] + [
        lax.ppermute(pieces[i], HEAD, [(j, j ^ i) for j in range(4)]) for i in range(1, 4)
    ]
    return lay(place, pieces)


def solution(mesh):
    fine = Mesh(mesh.devices.reshape(4, 2, 8, 2, 2), ("y", "xh", "z", "xl", "core"))
    ctx = ("y", "xh", "z")
    rows = P(ctx, HEAD, None)
    return jax.shard_map(
        per_device,
        mesh=fine,
        in_specs=(rows,) * 5 + (P(ctx),) * 3,
        out_specs=P(ctx + HEAD, None),
        check_vma=False,
    )
```

```python
import functools
import math

import jax
import jax.numpy as jnp
from jax import lax
from jax.experimental import pallas as pl
from jax.experimental.pallas import tpu as pltpu
from jax.sharding import Mesh, PartitionSpec as P

BLOCK = 128
SLOTS = 8
ROWS = SLOTS * BLOCK
TOK = 16
GROUP = 16
HD = 128
QR = TOK * GROUP
MEMBERS = 8
HEADS = 4
FAR = -1e30
SCALE = HD**-0.5 * math.log2(math.e)
VMEM = pl.BlockSpec(memory_space=pltpu.VMEM)
SMEM = pl.BlockSpec(memory_space=pltpu.SMEM)
ANY = pl.BlockSpec(memory_space=pl.ANY)
VALUES = ROWS
FRESH_K = 2 * ROWS
FRESH_V = FRESH_K + TOK
DESC = FRESH_V + TOK
PACK = DESC + TOK
CHAT, FILL, TOKEN_CHAT, INDEX = 0, 8, 16, 32
PIECE = QR // HEADS
SENT = PIECE + 16
WIDTHS = (2, 3, 5, 8)


def params():
    return pltpu.CompilerParams(vmem_limit_bytes=56 * 1024 * 1024)


def prepare_kernel(place, bc, bf, nc, q, k, v, nk, nv, pack, many, desc, sems):
    copies = [
        (k, pack.at[pl.ds(0, ROWS)]),
        (v, pack.at[pl.ds(VALUES, ROWS)]),
        (nk, pack.at[pl.ds(FRESH_K, TOK)]),
        (nv, pack.at[pl.ds(FRESH_V, TOK)]),
    ]
    copies += [(q, many.at[i, pl.ds(0, QR)]) for i in range(MEMBERS)]
    started = []
    for i, (src, dst) in enumerate(copies):
        copy = pltpu.make_async_copy(src, dst, sems.at[i])
        copy.start()
        started.append(copy)
    lane = lax.broadcasted_iota(jnp.int32, (TOK, HD), 1)
    row = jnp.where(lane == INDEX, place[0], 0)
    for i in range(SLOTS):
        row = jnp.where(lane == CHAT + i, bc[i], row)
        row = jnp.where(lane == FILL + i, bf[i], row)
    for i in range(TOK):
        row = jnp.where(lane == TOKEN_CHAT + i, nc[i], row)
    desc[...] = row.astype(jnp.float32).astype(jnp.bfloat16)
    copies = [(desc, pack.at[pl.ds(DESC, TOK)])]
    copies += [(desc, many.at[i, pl.ds(QR, TOK)]) for i in range(MEMBERS)]
    for i, (src, dst) in enumerate(copies):
        copy = pltpu.make_async_copy(src, dst, sems.at[4 + MEMBERS + i])
        copy.start()
        started.append(copy)
    for copy in started:
        copy.wait()


def prepare(place, bc, bf, nc, q, k, v, nk, nv):
    return pl.pallas_call(
        prepare_kernel,
        out_shape=[
            jax.ShapeDtypeStruct((PACK, HD), jnp.bfloat16),
            jax.ShapeDtypeStruct((MEMBERS, QR + TOK, HD), jnp.bfloat16),
        ],
        in_specs=[SMEM] * 4 + [ANY] * 5,
        out_specs=[ANY] * 2,
        scratch_shapes=[
            pltpu.VMEM((TOK, HD), jnp.bfloat16),
            pltpu.SemaphoreType.DMA((5 + 2 * MEMBERS,)),
        ],
        compiler_params=params(),
        name="prepare",
    )(place, bc, bf, nc, q, k, v, nk, nv)


def scores_of(q, keys):
    return lax.dot_general(q, keys, (((1,), (1,)), ((), ())), preferred_element_type=jnp.float32)


def attend_kernel(sources, split, first, last, *refs):
    refs = list(refs)
    take = lambda n: [refs.pop(0) for _ in range(n)]
    queries = take(1)[0]
    packs = take(sources + split)
    fresh = take(MEMBERS) if last else []
    state_in = (None, None) if first else tuple(take(2))
    out = take(1)[0] if last else None
    state_out = None if last else tuple(take(2))
    qa, rows_of, words, sem = take(4)
    ka, va = take(sources), take(sources)
    if last:
        na, nva, acc_last, ml_last = take(4)
        state_out = (acc_last, ml_last)

    def word_row(i, tile):
        rows_of[i : i + 1, :] = tile.astype(jnp.float32).astype(jnp.int32)[0:1, :]

    for i in range(MEMBERS):
        word_row(i, queries[i, QR : QR + TOK, :])
    for s in range(sources):
        tail = packs[s + split] if split else packs[s]
        word_row(MEMBERS + s, tail[tail.shape[0] - TOK :, :])
    if last:
        for i in range(MEMBERS):
            word_row(2 * MEMBERS + i, fresh[i][2 * TOK : 3 * TOK, :])
    copy = pltpu.make_async_copy(rows_of, words, sem)
    copy.start()

    for s in range(sources):
        if split:
            ka[s][:, 0:HD] = packs[0][...]
            va[s][:, 0:HD] = packs[1][0:ROWS, :]
        else:
            ka[s][:, 0:HD] = packs[s][0:ROWS, :]
            va[s][:, 0:HD] = packs[s][VALUES : VALUES + ROWS, :]
        va[s][:, HD : 2 * HD] = jnp.ones((ROWS, HD), jnp.bfloat16)
    copy.wait()

    lane = lax.broadcasted_iota(jnp.int32, (TOK, HD), 1)
    for i in range(MEMBERS):
        qa[i * QR : (i + 1) * QR, 0:HD] = queries[i, 0:QR, :]
        for t in range(TOK):
            rows = slice(i * QR + t * GROUP, i * QR + (t + 1) * GROUP)
            hot = jnp.where(lane == words[i, TOKEN_CHAT + t], 1.0, 0.0)
            qa[rows, HD : 2 * HD] = hot.astype(jnp.bfloat16)
    lane = lax.broadcasted_iota(jnp.int32, (BLOCK, HD), 1)
    row = lax.broadcasted_iota(jnp.int32, (BLOCK, HD), 0)
    for s in range(sources):
        for slot in range(SLOTS):
            live = (lane == words[MEMBERS + s, CHAT + slot]) & (row < words[MEMBERS + s, FILL + slot])
            at = slice(slot * BLOCK, (slot + 1) * BLOCK)
            ka[s][at, HD : 2 * HD] = jnp.where(live, 0.0, FAR).astype(jnp.bfloat16)
    if last:
        lane = lax.broadcasted_iota(jnp.int32, (TOK, HD), 1)
        row = lax.broadcasted_iota(jnp.int32, (TOK, HD), 0)
        key_lane = lax.broadcasted_iota(jnp.int32, (1, HD), 1)
        key_pos = jnp.zeros((1, HD), jnp.int32)
        for i in range(MEMBERS):
            at = slice(i * TOK, (i + 1) * TOK)
            na[at, 0:HD] = fresh[i][0:TOK, :]
            nva[at, 0:HD] = fresh[i][TOK : 2 * TOK, :]
            chat = jnp.zeros((TOK, HD), jnp.int32)
            for t in range(TOK):
                chat = jnp.where(row == t, words[2 * MEMBERS + i, TOKEN_CHAT + t], chat)
            na[at, HD : 2 * HD] = jnp.where(lane == chat, 0.0, FAR).astype(jnp.bfloat16)
            start = words[2 * MEMBERS + i, INDEX] * TOK
            key_pos = jnp.where(key_lane // TOK == i, start + key_lane % TOK, key_pos)
        nva[:, HD : 2 * HD] = jnp.ones((BLOCK, HD), jnp.bfloat16)

    half_lane = lax.broadcasted_iota(jnp.int32, (QR, HD), 1) < HD // 2

    def fold(rows, pieces):
        top = None
        for scores, _ in pieces:
            for j in range(scores.shape[1] // HD):
                tile = scores[:, j * HD : (j + 1) * HD]
                top = tile if top is None else jnp.maximum(top, tile)
        new = jnp.max(top, axis=1, keepdims=True)
        if not first:
            stats = state_in[1][rows, :]
            old, total = stats[:, 0:1], stats[:, HD // 2 : HD // 2 + 1]
            new = jnp.maximum(old, new)
        summed = None
        for scores, values in pieces:
            weights = jnp.exp2((scores - new) * SCALE).astype(jnp.bfloat16)
            product = jnp.dot(weights, values, preferred_element_type=jnp.float32)
            summed = product if summed is None else summed + product
        acc, total_now = summed[:, 0:HD], summed[:, HD : 2 * HD]
        if not first:
            factor = jnp.exp2((old - new) * SCALE)
            acc = acc + state_in[0][rows, :] * factor
            total_now = total_now + total * factor
        state_out[0][rows, :] = acc
        state_out[1][rows, :] = jnp.where(half_lane, new, total_now)

    def chunk(c, carry):
        rows = pl.ds(pl.multiple_of(c * QR, QR), QR)
        low, high = words[c, TOKEN_CHAT], words[c, TOKEN_CHAT + TOK - 1]
        begins, count = [], jnp.int32(0)
        for s in range(sources):
            begin, end = jnp.int32(0), jnp.int32(0)
            for slot in range(SLOTS):
                chat = words[MEMBERS + s, CHAT + slot]
                begin += (chat < low).astype(jnp.int32)
                end += (chat <= high).astype(jnp.int32)
            begins.append(begin)
            count = jnp.maximum(count, end - begin)

        def step(slots):
            q = qa[rows, :]
            pieces = []
            for s in range(sources):
                at = pl.multiple_of(jnp.minimum(begins[s], SLOTS - slots) * BLOCK, BLOCK)
                at = pl.ds(at, slots * BLOCK)
                pieces.append((scores_of(q, ka[s][at, :]), va[s][at, :]))
            if last:
                token = lax.broadcasted_iota(jnp.int32, (QR, HD), 0) // GROUP
                seen = key_pos <= words[c, INDEX] * TOK + token
                pieces.append((jnp.where(seen, scores_of(q, na[...]), FAR), nva[...]))
            fold(rows, pieces)

        under = 0
        for slots in WIDTHS:
            fits = count <= slots if under == 0 else (count > under) & (count <= slots)
            pl.when(fits)(functools.partial(step, slots))
            under = slots
        return carry

    lax.fori_loop(0, MEMBERS, chunk, 0)

    if last:
        row = lax.broadcasted_iota(jnp.int32, (16, HD), 0)

        def finish(c, carry):
            rows = pl.ds(pl.multiple_of(c * QR, QR), QR)
            stats = state_out[1][rows, :]
            total = stats[:, HD // 2 : HD // 2 + 1]
            normal = (state_out[0][rows, :] / total).astype(jnp.bfloat16)
            sums = jnp.broadcast_to(stats[:, 0:1] * SCALE + jnp.log2(total), (QR, HD)).T
            for j in range(HEADS):
                piece = c * HEADS + j
                out[piece, 0:PIECE, :] = normal[j * PIECE : (j + 1) * PIECE, :]
                line = sums[0:16, (j // 2) * HD : (j // 2 + 1) * HD]
                top = line.astype(jnp.bfloat16).astype(jnp.float32)
                rest = line - top
                middle = rest.astype(jnp.bfloat16).astype(jnp.float32)
                low = rest - middle
                terms = jnp.where(row == 0, top, jnp.where(row == 1, middle, low))
                out[piece, PIECE:SENT, :] = terms.astype(jnp.bfloat16)
            return carry

        lax.fori_loop(0, MEMBERS, finish, 0)


def attend(queries, packs, fresh, state, last=False):
    split = 1 if last else 0
    sources, first = len(packs) - split, state is None
    operands = [queries, *packs, *fresh]
    specs = [VMEM] * (1 + len(packs))
    fresh_rows = 3 * TOK
    for x in fresh:
        at = (x.shape[0] - fresh_rows) // TOK
        specs += [pl.BlockSpec((pl.Element(fresh_rows), pl.Element(HD)), lambda i, at=at: (at * TOK, 0))]
    if not first:
        operands += state
        specs += [VMEM, VMEM]
    rows = MEMBERS * QR
    state_shape = jax.ShapeDtypeStruct((rows, HD), jnp.float32)
    if last:
        out_shape = jax.ShapeDtypeStruct((MEMBERS * HEADS, SENT, HD), jnp.bfloat16)
    else:
        out_shape = [state_shape] * 2
    scratch = [
        pltpu.VMEM((rows, 2 * HD), jnp.bfloat16),
        pltpu.VMEM((3 * MEMBERS, HD), jnp.int32),
        pltpu.SMEM((3 * MEMBERS, HD), jnp.int32),
        pltpu.SemaphoreType.DMA,
    ]
    scratch += [pltpu.VMEM((ROWS, 2 * HD), jnp.bfloat16)] * (2 * sources)
    if last:
        scratch += [pltpu.VMEM((BLOCK, 2 * HD), jnp.bfloat16)] * 2
        scratch += [pltpu.VMEM((rows, HD), jnp.float32)] * 2
    return pl.pallas_call(
        functools.partial(attend_kernel, sources, split, first, last),
        grid=(1,),
        out_shape=out_shape,
        in_specs=specs,
        out_specs=VMEM if last else [VMEM] * 2,
        scratch_shapes=scratch,
        compiler_params=params(),
        cost_estimate=pl.CostEstimate(
            flops=sources * 4 * rows * ROWS * HD,
            bytes_accessed=sources * ROWS * HD * 4 + rows * HD * 18,
            transcendentals=sources * rows * ROWS,
        ),
        name="attend_last" if last else "attend",
    )(*operands)


def finish_kernel(place, parts, out, turned, held):
    top = None
    lines = []
    for z in range(MEMBERS):
        rows = []
        for h in range(HEADS):
            terms = parts[z * HEADS + h, PIECE:SENT, :].astype(jnp.float32)
            rows.append(terms[0:1, :] + terms[1:2, :] + terms[2:3, :])
        lines.append(rows)
    shares = [[None] * HEADS for _ in range(MEMBERS)]
    for h in range(HEADS):
        top = lines[0][h]
        for z in range(1, MEMBERS):
            top = jnp.maximum(top, lines[z][h])
        powers = [jnp.exp2(lines[z][h] - top) for z in range(MEMBERS)]
        whole = powers[0]
        for power in powers[1:]:
            whole = whole + power
        for z in range(MEMBERS):
            shares[z][h] = powers[z] / whole
    for z in range(MEMBERS):
        for h in range(HEADS):
            at = z * HEADS + h
            turned[at : at + 1, :] = shares[z][h]
    held[...] = turned[...].T
    at = pl.multiple_of(lax.rem(place[1], 2) * PIECE, PIECE)
    columns = held[pl.ds(at, PIECE), :]
    for h in range(HEADS):
        total = None
        for z in range(MEMBERS):
            i = z * HEADS + h
            term = parts[i, 0:PIECE, :].astype(jnp.float32) * columns[:, i : i + 1]
            total = term if total is None else total + term
        turned[0:PIECE, :] = total
        for g in range(GROUP):
            at = (h * GROUP + g) * HD
            out[:, at : at + HD] = turned[pl.ds(g, TOK // HEADS, stride=GROUP), :].astype(jnp.bfloat16)


def finish(place, parts):
    return pl.pallas_call(
        finish_kernel,
        out_shape=jax.ShapeDtypeStruct((TOK // HEADS, HEADS * GROUP * HD), jnp.bfloat16),
        in_specs=[SMEM, VMEM],
        out_specs=VMEM,
        scratch_shapes=[pltpu.VMEM((HD, HD), jnp.float32)] * 2,
        compiler_params=params(),
        name="finish",
    )(place, parts)


YX = ("y", "xh")
HEAD = ("xl", "core")


def up(x):
    return lax.ppermute(x, "y", [(i, (i + 1) % 4) for i in range(4)])


def down(x):
    return lax.ppermute(x, "y", [(i, (i - 1) % 4) for i in range(4)])


def across(x):
    return lax.ppermute(x, "xh", [(0, 1), (1, 0)])


def per_device(queries, cache_keys, cache_values, new_keys, new_values, block_chat, block_fill, new_chat):
    place = jnp.stack([lax.axis_index(("y", "xh", "z")), lax.axis_index(HEAD)]).astype(jnp.int32)
    mine, many = prepare(
        place,
        block_chat,
        block_fill,
        new_chat,
        queries.reshape(QR, HD),
        cache_keys[:, 0, :],
        cache_values[:, 0, :],
        new_keys[:, 0, :],
        new_values[:, 0, :],
    )
    before, after, beside = up(mine), down(mine), across(mine)
    shared = lax.all_to_all(many, "z", split_axis=0, concat_axis=0, tiled=True)
    state = attend(shared, [mine], [], None)
    beside_before, opposite, beside_after = up(beside), down(after), across(after)
    state = attend(shared, [before, after, beside], [], state)
    far_keys = across(opposite[:ROWS])
    far_rest = up(beside_before[VALUES:])
    state = attend(shared, [beside_before, opposite, beside_after], [], state)
    fresh = [mine, before, after, beside, beside_before, opposite, beside_after, far_rest]
    parts = attend(shared, [far_keys, far_rest], fresh, state, last=True)
    parts = lax.all_to_all(parts, ("z",) + HEAD, split_axis=0, concat_axis=0, tiled=True)
    return finish(place, parts)


def solution(mesh):
    fine = Mesh(mesh.devices.reshape(4, 2, 8, 2, 2), ("y", "xh", "z", "xl", "core"))
    ctx = ("y", "xh", "z")
    rows = P(ctx, HEAD, None)
    return jax.shard_map(
        per_device,
        mesh=fine,
        in_specs=(rows,) * 5 + (P(ctx),) * 3,
        out_specs=P(ctx + HEAD, None),
        check_vma=False,
    )
```

```python
import functools
import math

import jax
import jax.numpy as jnp
from jax import lax
from jax.experimental import pallas as pl
from jax.experimental.pallas import tpu as pltpu
from jax.sharding import Mesh, PartitionSpec as P

BLOCK = 128
SLOTS = 8
ROWS = SLOTS * BLOCK
TOK = 16
GROUP = 16
HD = 128
QR = TOK * GROUP
MEMBERS = 8
HEADS = 4
FAR = -1e30
SCALE = HD**-0.5 * math.log2(math.e)
VMEM = pl.BlockSpec(memory_space=pltpu.VMEM)
SMEM = pl.BlockSpec(memory_space=pltpu.SMEM)
VALUES = ROWS
FRESH_K = 2 * ROWS
FRESH_V = FRESH_K + TOK
DESC = FRESH_V + TOK
PACK = DESC + TOK
CHAT, FILL, TOKEN_CHAT, INDEX = 0, 8, 16, 32
PIECE = QR // HEADS
SENT = PIECE + 16
WIDTHS = (2, 3, 4, 6, 8)
TILE = 4
HIGHEST = 2.0**80


def params():
    return pltpu.CompilerParams(vmem_limit_bytes=36 * 1024 * 1024)


def prepare_kernel(place, bc, bf, nc, q, k, v, nk, nv, pack, many):
    lane = lax.broadcasted_iota(jnp.int32, (TOK, HD), 1)
    row = jnp.where(lane == INDEX, place[0], 0)
    for i in range(SLOTS):
        row = jnp.where(lane == CHAT + i, bc[i], row)
        row = jnp.where(lane == FILL + i, bf[i], row)
    for i in range(TOK):
        row = jnp.where(lane == TOKEN_CHAT + i, nc[i], row)
    desc = row.astype(jnp.float32).astype(jnp.bfloat16)
    pack[0:ROWS, :] = k[...]
    pack[VALUES : VALUES + ROWS, :] = v[...]
    pack[FRESH_K : FRESH_K + TOK, :] = nk[...]
    pack[FRESH_V : FRESH_V + TOK, :] = nv[...]
    pack[DESC:PACK, :] = desc
    for i in range(MEMBERS):
        many[i, 0:QR, :] = q[...]
        many[i, QR : QR + TOK, :] = desc


def prepare(place, bc, bf, nc, q, k, v, nk, nv):
    return pl.pallas_call(
        prepare_kernel,
        out_shape=[
            jax.ShapeDtypeStruct((PACK, HD), jnp.bfloat16),
            jax.ShapeDtypeStruct((MEMBERS, QR + TOK, HD), jnp.bfloat16),
        ],
        in_specs=[SMEM] * 4 + [VMEM] * 5,
        out_specs=[VMEM] * 2,
        compiler_params=params(),
        name="prepare",
    )(place, bc, bf, nc, q, k, v, nk, nv)


def scores_of(q, keys):
    return lax.dot_general(q, keys, (((1,), (1,)), ((), ())), preferred_element_type=jnp.float32)


def attend_kernel(sources, first, last, *refs):
    refs = list(refs)
    take = lambda n: [refs.pop(0) for _ in range(n)]
    queries = take(1)[0]
    packs = take(sources)
    fresh = take(MEMBERS) if last else []
    state_in = None if first else tuple(take(2))
    out = take(1)[0] if last else None
    state_out = None if last else tuple(take(2))
    qa, rows_of, words, sem = take(4)
    ka, va = take(sources), take(sources)
    if last:
        na, nva, sums_last, tops_last = take(4)
        state_out = (sums_last, tops_last)

    def word_row(i, tile):
        rows_of[i : i + 1, :] = tile.astype(jnp.float32).astype(jnp.int32)[0:1, :]

    for i in range(MEMBERS):
        word_row(i, queries[i, QR : QR + TOK, :])
    for s in range(sources):
        word_row(MEMBERS + s, packs[s][DESC:PACK, :])
    if last:
        for i in range(MEMBERS):
            word_row(2 * MEMBERS + i, fresh[i][2 * TOK : 3 * TOK, :])
    copy = pltpu.make_async_copy(rows_of, words, sem)
    copy.start()

    for s in range(sources):
        ka[s][:, 0:HD] = packs[s][0:ROWS, :]
        va[s][:, 0:HD] = packs[s][VALUES : VALUES + ROWS, :]
        va[s][:, HD : 2 * HD] = jnp.ones((ROWS, HD), jnp.bfloat16)
    copy.wait()

    lane = lax.broadcasted_iota(jnp.int32, (TOK, HD), 1)
    for i in range(MEMBERS):
        qa[i * QR : (i + 1) * QR, 0:HD] = queries[i, 0:QR, :]
        for t in range(TOK):
            rows = slice(i * QR + t * GROUP, i * QR + (t + 1) * GROUP)
            hot = jnp.where(lane == words[i, TOKEN_CHAT + t], 1.0, 0.0)
            qa[rows, HD : 2 * HD] = hot.astype(jnp.bfloat16)
    lane = lax.broadcasted_iota(jnp.int32, (BLOCK, HD), 1)
    row = lax.broadcasted_iota(jnp.int32, (BLOCK, HD), 0)
    for s in range(sources):
        for slot in range(SLOTS):
            live = (lane == words[MEMBERS + s, CHAT + slot]) & (row < words[MEMBERS + s, FILL + slot])
            at = slice(slot * BLOCK, (slot + 1) * BLOCK)
            ka[s][at, HD : 2 * HD] = jnp.where(live, 0.0, FAR).astype(jnp.bfloat16)
    if last:
        lane = lax.broadcasted_iota(jnp.int32, (TOK, HD), 1)
        row = lax.broadcasted_iota(jnp.int32, (TOK, HD), 0)
        key_lane = lax.broadcasted_iota(jnp.int32, (1, HD), 1)
        key_pos = jnp.zeros((1, HD), jnp.int32)
        for i in range(MEMBERS):
            at = slice(i * TOK, (i + 1) * TOK)
            na[at, 0:HD] = fresh[i][0:TOK, :]
            nva[at, 0:HD] = fresh[i][TOK : 2 * TOK, :]
            chat = jnp.zeros((TOK, HD), jnp.int32)
            for t in range(TOK):
                chat = jnp.where(row == t, words[2 * MEMBERS + i, TOKEN_CHAT + t], chat)
            na[at, HD : 2 * HD] = jnp.where(lane == chat, 0.0, FAR).astype(jnp.bfloat16)
            start = words[2 * MEMBERS + i, INDEX] * TOK
            key_pos = jnp.where(key_lane // TOK == i, start + key_lane % TOK, key_pos)
        nva[:, HD : 2 * HD] = jnp.ones((BLOCK, HD), jnp.bfloat16)

    def exact(state, rows, pieces):
        pieces = [(scores(), values()) for scores, values in pieces]
        top = None
        for scores, _ in pieces:
            for j in range(scores.shape[1] // HD):
                tile = scores[:, j * HD : (j + 1) * HD]
                top = tile if top is None else jnp.maximum(top, tile)
        new = jnp.broadcast_to(jnp.max(top, axis=1, keepdims=True), top.shape)
        if state is not None:
            old = state[1][rows, :]
            new = jnp.maximum(old, new)
        summed = None
        for scores, values in pieces:
            shift = jnp.concatenate([new] * (scores.shape[1] // HD), axis=1)
            weights = jnp.exp2((scores - shift) * SCALE).astype(jnp.bfloat16)
            product = jnp.dot(weights, values, preferred_element_type=jnp.float32)
            summed = product if summed is None else summed + product
        if state is not None:
            factor = jnp.exp2((old - new) * SCALE)
            summed = summed + state[0][rows, :] * jnp.concatenate([factor, factor], axis=1)
        state_out[0][rows, :] = summed
        state_out[1][rows, :] = new

    def fold(state, rows, pieces):
        shift = state[1][rows, :]
        scaled = shift * SCALE
        summed = state[0][rows, :]
        for scores, values in pieces:
            scores = scores()
            wide = jnp.concatenate([scaled] * (scores.shape[1] // HD), axis=1)
            weights = jnp.exp2(scores * SCALE - wide).astype(jnp.bfloat16)
            summed = summed + jnp.dot(weights, values(), preferred_element_type=jnp.float32)
        fine = jnp.max(summed[:, HD : 2 * HD]) < HIGHEST

        @pl.when(fine)
        def _():
            state_out[0][rows, :] = summed
            if state is not state_out:
                state_out[1][rows, :] = shift

        @pl.when(jnp.logical_not(fine))
        def _():
            exact(state, rows, pieces)

    def chunk(i, carry):
        c = i * TILE
        rows = pl.ds(pl.multiple_of(c * QR, QR), TILE * QR)
        low, high = words[c, TOKEN_CHAT], words[c + TILE - 1, TOKEN_CHAT + TOK - 1]

        def part(members, state, fresh_too):
            begins, count = [], jnp.int32(0)
            for s in members:
                begin, end = jnp.int32(0), jnp.int32(0)
                for slot in range(SLOTS):
                    chat = words[MEMBERS + s, CHAT + slot]
                    begin += (chat < low).astype(jnp.int32)
                    end += (chat <= high).astype(jnp.int32)
                begins.append(begin)
                count = jnp.maximum(count, end - begin)

            def step(slots):
                pieces = []
                for s, begin in zip(members, begins):
                    at = pl.multiple_of(jnp.minimum(begin, SLOTS - slots) * BLOCK, BLOCK)
                    at = pl.ds(at, slots * BLOCK)
                    pieces.append(
                        (
                            lambda s=s, at=at: scores_of(qa[rows, :], ka[s][at, :]),
                            lambda s=s, at=at: va[s][at, :],
                        )
                    )
                if fresh_too:

                    def fresh_scores():
                        token = lax.broadcasted_iota(jnp.int32, (TILE * QR, HD), 0) // GROUP
                        seen = key_pos <= words[c, INDEX] * TOK + token
                        return jnp.where(seen, scores_of(qa[rows, :], na[...]), FAR)

                    pieces.append((fresh_scores, lambda: nva[...]))
                if state is None:
                    exact(None, rows, pieces)
                else:
                    fold(state, rows, pieces)

            under = 0
            for slots in WIDTHS:
                fits = count <= slots if under == 0 else (count > under) & (count <= slots)
                pl.when(fits)(functools.partial(step, slots))
                under = slots

        if first:
            part([0], None, False)
            part(range(1, sources), state_out, False)
        else:
            part(range(sources), state_in, last)
        return carry

    lax.fori_loop(0, MEMBERS // TILE, chunk, 0)

    if last:
        row = lax.broadcasted_iota(jnp.int32, (16, HD), 0)

        def close(c, carry):
            rows = pl.ds(pl.multiple_of(c * QR, QR), QR)
            sums = state_out[0][rows, :]
            total = sums[:, HD : 2 * HD]
            normal = (sums[:, 0:HD] / total).astype(jnp.bfloat16)
            logs = (state_out[1][rows, :] * SCALE + jnp.log2(total)).T
            for j in range(HEADS):
                piece = c * HEADS + j
                out[piece, 0:PIECE, :] = normal[j * PIECE : (j + 1) * PIECE, :]
                line = logs[0:16, (j // 2) * HD : (j // 2 + 1) * HD]
                top = line.astype(jnp.bfloat16).astype(jnp.float32)
                rest = line - top
                middle = rest.astype(jnp.bfloat16).astype(jnp.float32)
                low = rest - middle
                terms = jnp.where(row == 0, top, jnp.where(row == 1, middle, low))
                out[piece, PIECE:SENT, :] = terms.astype(jnp.bfloat16)
            return carry

        lax.fori_loop(0, MEMBERS, close, 0)


def attend(queries, packs, fresh, state, last=False):
    sources, first = len(packs), state is None
    operands = [queries, *packs, *fresh]
    specs = [VMEM] * (1 + sources)
    tail = pl.BlockSpec((pl.Element(3 * TOK), pl.Element(HD)), lambda i: (FRESH_K, 0))
    specs += [tail] * len(fresh)
    if not first:
        operands += state
        specs += [VMEM, VMEM]
    rows = MEMBERS * QR
    state_shapes = [(rows, 2 * HD), (rows, HD)]
    if last:
        out_shape = jax.ShapeDtypeStruct((MEMBERS * HEADS, SENT, HD), jnp.bfloat16)
    else:
        out_shape = [jax.ShapeDtypeStruct(s, jnp.float32) for s in state_shapes]
    scratch = [
        pltpu.VMEM((rows, 2 * HD), jnp.bfloat16),
        pltpu.VMEM((3 * MEMBERS, HD), jnp.int32),
        pltpu.SMEM((3 * MEMBERS, HD), jnp.int32),
        pltpu.SemaphoreType.DMA,
    ]
    scratch += [pltpu.VMEM((ROWS, 2 * HD), jnp.bfloat16)] * (2 * sources)
    if last:
        scratch += [pltpu.VMEM((BLOCK, 2 * HD), jnp.bfloat16)] * 2
        scratch += [pltpu.VMEM(s, jnp.float32) for s in state_shapes]
    return pl.pallas_call(
        functools.partial(attend_kernel, sources, first, last),
        grid=(1,),
        out_shape=out_shape,
        in_specs=specs,
        out_specs=VMEM if last else [VMEM] * 2,
        scratch_shapes=scratch,
        compiler_params=params(),
        cost_estimate=pl.CostEstimate(
            flops=sources * 4 * rows * ROWS * HD,
            bytes_accessed=sources * ROWS * HD * 4 + rows * HD * 18,
            transcendentals=sources * rows * ROWS,
        ),
        name="attend_last" if last else "attend",
    )(*operands)


def finish_kernel(place, parts, out, turned, held):
    top = None
    lines = []
    for z in range(MEMBERS):
        rows = []
        for h in range(HEADS):
            terms = parts[z * HEADS + h, PIECE:SENT, :].astype(jnp.float32)
            rows.append(terms[0:1, :] + terms[1:2, :] + terms[2:3, :])
        lines.append(rows)
    shares = [[None] * HEADS for _ in range(MEMBERS)]
    for h in range(HEADS):
        top = lines[0][h]
        for z in range(1, MEMBERS):
            top = jnp.maximum(top, lines[z][h])
        powers = [jnp.exp2(lines[z][h] - top) for z in range(MEMBERS)]
        whole = powers[0]
        for power in powers[1:]:
            whole = whole + power
        for z in range(MEMBERS):
            shares[z][h] = powers[z] / whole
    for z in range(MEMBERS):
        for h in range(HEADS):
            at = z * HEADS + h
            turned[at : at + 1, :] = shares[z][h]
    held[...] = turned[...].T
    at = pl.multiple_of(lax.rem(place[1], 2) * PIECE, PIECE)
    columns = held[pl.ds(at, PIECE), :]
    for h in range(HEADS):
        total = None
        for z in range(MEMBERS):
            i = z * HEADS + h
            term = parts[i, 0:PIECE, :].astype(jnp.float32) * columns[:, i : i + 1]
            total = term if total is None else total + term
        turned[0:PIECE, :] = total
        for g in range(GROUP):
            at = (h * GROUP + g) * HD
            out[:, at : at + HD] = turned[pl.ds(g, TOK // HEADS, stride=GROUP), :].astype(jnp.bfloat16)


def finish(place, parts):
    return pl.pallas_call(
        finish_kernel,
        out_shape=jax.ShapeDtypeStruct((TOK // HEADS, HEADS * GROUP * HD), jnp.bfloat16),
        in_specs=[SMEM, VMEM],
        out_specs=VMEM,
        scratch_shapes=[pltpu.VMEM((HD, HD), jnp.float32)] * 2,
        compiler_params=params(),
        name="finish",
    )(place, parts)


YX = ("y", "xh")
HEAD = ("xl", "core")


def up(x):
    return lax.ppermute(x, "y", [(i, (i + 1) % 4) for i in range(4)])


def down(x):
    return lax.ppermute(x, "y", [(i, (i - 1) % 4) for i in range(4)])


def across(x):
    return lax.ppermute(x, "xh", [(0, 1), (1, 0)])


def per_device(queries, cache_keys, cache_values, new_keys, new_values, block_chat, block_fill, new_chat):
    place = jnp.stack([lax.axis_index(("y", "xh", "z")), lax.axis_index(HEAD)]).astype(jnp.int32)
    mine, many = prepare(
        place,
        block_chat,
        block_fill,
        new_chat,
        queries.reshape(QR, HD),
        cache_keys[:, 0, :],
        cache_values[:, 0, :],
        new_keys[:, 0, :],
        new_values[:, 0, :],
    )
    before, after, beside = up(mine), down(mine), across(mine)
    shared = lax.all_to_all(many, "z", split_axis=0, concat_axis=0, tiled=True)
    beside_before, opposite, beside_after = up(beside), down(after), across(after)
    state = attend(shared, [mine, before, after, beside], [], None)
    far = across(opposite)
    state = attend(shared, [beside_before, opposite, beside_after], [], state)
    fresh = [mine, before, after, beside, beside_before, opposite, beside_after, far]
    parts = attend(shared, [far], fresh, state, last=True)
    parts = lax.all_to_all(parts, ("z",) + HEAD, split_axis=0, concat_axis=0, tiled=True)
    return finish(place, parts)


def solution(mesh):
    fine = Mesh(mesh.devices.reshape(4, 2, 8, 2, 2), ("y", "xh", "z", "xl", "core"))
    ctx = ("y", "xh", "z")
    rows = P(ctx, HEAD, None)
    return jax.shard_map(
        per_device,
        mesh=fine,
        in_specs=(rows,) * 5 + (P(ctx),) * 3,
        out_specs=P(ctx + HEAD, None),
        check_vma=False,
    )
```

```python
import functools
import math

import jax
import jax.numpy as jnp
from jax import lax
from jax.experimental import pallas as pl
from jax.experimental.pallas import tpu as pltpu
from jax.sharding import Mesh, PartitionSpec as P

BLOCK = 128
SLOTS = 8
ROWS = SLOTS * BLOCK
TOK = 16
GROUP = 16
HD = 128
QR = TOK * GROUP
MEMBERS = 8
HEADS = 4
FAR = -1e30
SCALE = HD**-0.5 * math.log2(math.e)
VMEM = pl.BlockSpec(memory_space=pltpu.VMEM)
SMEM = pl.BlockSpec(memory_space=pltpu.SMEM)
ANY = pl.BlockSpec(memory_space=pl.ANY)
VALUES = ROWS
FRESH_K = 2 * ROWS
FRESH_V = FRESH_K + TOK
DESC = FRESH_V + TOK
PACK = DESC + TOK
SHARED = QR + 2 * TOK
CHAT, FILL, TOKEN_CHAT, INDEX = 0, 8, 16, 32
PIECE = QR // HEADS
SENT = PIECE + 16
WIDTHS = (2, 3, 4, 6, 8)
TILE = 4
HIGHEST = 2.0**80
LOWEST = 2.0**-120


def params():
    return pltpu.CompilerParams(vmem_limit_bytes=36 * 1024 * 1024)


def prepare_kernel(place, bc, bf, nc, q, k, v, nk, nv, pack, many, sems):
    copies = [
        (k, pack.at[pl.ds(0, ROWS)]),
        (v, pack.at[pl.ds(VALUES, ROWS)]),
        (nk, pack.at[pl.ds(FRESH_K, TOK)]),
        (nv, pack.at[pl.ds(FRESH_V, TOK)]),
        (q, many.at[0, pl.ds(0, QR)]),
    ]
    started = []
    for i, (src, dst) in enumerate(copies):
        copy = pltpu.make_async_copy(src, dst, sems.at[i])
        copy.start()
        started.append(copy)
    lane = lax.broadcasted_iota(jnp.int32, (TOK, HD), 1)
    row = jnp.where(lane == INDEX, place[0], 0)
    for i in range(SLOTS):
        row = jnp.where(lane == CHAT + i, bc[i], row)
        row = jnp.where(lane == FILL + i, bf[i], row)
    for i in range(TOK):
        row = jnp.where(lane == TOKEN_CHAT + i, nc[i], row)
    desc = row.astype(jnp.float32).astype(jnp.bfloat16)
    pack[DESC:PACK, :] = desc
    for copy in started:
        copy.wait()
    own = pack[FRESH_K : FRESH_K + TOK, :]
    for i in range(MEMBERS):
        if i > 0:
            many[i, 0:QR, :] = many[0, 0:QR, :]
        many[i, QR : QR + TOK, :] = own
        many[i, QR + TOK : SHARED, :] = desc


def prepare(place, bc, bf, nc, q, k, v, nk, nv):
    return pl.pallas_call(
        prepare_kernel,
        out_shape=[
            jax.ShapeDtypeStruct((PACK, HD), jnp.bfloat16),
            jax.ShapeDtypeStruct((MEMBERS, SHARED, HD), jnp.bfloat16),
        ],
        in_specs=[SMEM] * 4 + [ANY] * 5,
        out_specs=[VMEM] * 2,
        scratch_shapes=[pltpu.SemaphoreType.DMA((5,))],
        compiler_params=pltpu.CompilerParams(vmem_limit_bytes=58 * 1024 * 1024),
        name="prepare",
    )(place, bc, bf, nc, q, k, v, nk, nv)


def scores_of(q, keys):
    return lax.dot_general(q, keys, (((1,), (1,)), ((), ())), preferred_element_type=jnp.float32)


def attend_kernel(sources, first, last, *refs):
    refs = list(refs)
    take = lambda n: [refs.pop(0) for _ in range(n)]
    queries = take(1)[0]
    packs = take(sources)
    fresh = take(MEMBERS) if last else []
    state_in = None if first else tuple(take(2))
    out = take(1)[0] if last else None
    state_out = None if last else tuple(take(2))
    qa, rows_of, words, sem = take(4)
    ka, va = take(sources), take(sources)
    if last:
        na, nva, sums_last, tops_last = take(4)
        state_out = (sums_last, tops_last)

    def word_row(i, tile):
        rows_of[i : i + 1, :] = tile.astype(jnp.float32).astype(jnp.int32)[0:1, :]

    for i in range(MEMBERS):
        word_row(i, queries[i, QR + TOK : SHARED, :])
    for s in range(sources):
        word_row(MEMBERS + s, packs[s][DESC:PACK, :])
    if last:
        for i in range(MEMBERS):
            word_row(2 * MEMBERS + i, fresh[i][2 * TOK : 3 * TOK, :])
    copy = pltpu.make_async_copy(rows_of, words, sem)
    copy.start()

    for s in range(sources):
        ka[s][:, 0:HD] = packs[s][0:ROWS, :]
        va[s][:, 0:HD] = packs[s][VALUES : VALUES + ROWS, :]
        va[s][:, HD : 2 * HD] = jnp.ones((ROWS, HD), jnp.bfloat16)
    copy.wait()

    lane = lax.broadcasted_iota(jnp.int32, (TOK, HD), 1)
    for i in range(MEMBERS):
        qa[i * QR : (i + 1) * QR, 0:HD] = queries[i, 0:QR, :]
        for t in range(TOK):
            rows = slice(i * QR + t * GROUP, i * QR + (t + 1) * GROUP)
            hot = jnp.where(lane == words[i, TOKEN_CHAT + t], 1.0, 0.0)
            qa[rows, HD : 2 * HD] = hot.astype(jnp.bfloat16)
    lane = lax.broadcasted_iota(jnp.int32, (BLOCK, HD), 1)
    row = lax.broadcasted_iota(jnp.int32, (BLOCK, HD), 0)
    for s in range(sources):
        for slot in range(SLOTS):
            live = (lane == words[MEMBERS + s, CHAT + slot]) & (row < words[MEMBERS + s, FILL + slot])
            at = slice(slot * BLOCK, (slot + 1) * BLOCK)
            ka[s][at, HD : 2 * HD] = jnp.where(live, 0.0, FAR).astype(jnp.bfloat16)
    if last:
        lane = lax.broadcasted_iota(jnp.int32, (TOK, HD), 1)
        row = lax.broadcasted_iota(jnp.int32, (TOK, HD), 0)
        key_lane = lax.broadcasted_iota(jnp.int32, (1, HD), 1)
        key_pos = jnp.zeros((1, HD), jnp.int32)
        for i in range(MEMBERS):
            at = slice(i * TOK, (i + 1) * TOK)
            na[at, 0:HD] = fresh[i][0:TOK, :]
            nva[at, 0:HD] = fresh[i][TOK : 2 * TOK, :]
            chat = jnp.zeros((TOK, HD), jnp.int32)
            for t in range(TOK):
                chat = jnp.where(row == t, words[2 * MEMBERS + i, TOKEN_CHAT + t], chat)
            na[at, HD : 2 * HD] = jnp.where(lane == chat, 0.0, FAR).astype(jnp.bfloat16)
            start = words[2 * MEMBERS + i, INDEX] * TOK
            key_pos = jnp.where(key_lane // TOK == i, start + key_lane % TOK, key_pos)
        nva[:, HD : 2 * HD] = jnp.ones((BLOCK, HD), jnp.bfloat16)

    def fresh_scores(rows, c):
        token = lax.broadcasted_iota(jnp.int32, (TILE * QR, HD), 0) // GROUP
        seen = key_pos <= words[c, INDEX] * TOK + token
        return jnp.where(seen, scores_of(qa[rows, :], na[...]), FAR)

    def exact(state, shift, rows, c, members, fresh_too):
        sums, tops = state_out
        if state is None:
            sums[rows, :] = jnp.zeros((TILE * QR, 2 * HD), jnp.float32)
            tops[rows, :] = shift
        elif state is not state_out:
            sums[rows, :] = state[0][rows, :]
            tops[rows, :] = shift

        def block(scores, values):
            old = tops[rows, :]
            new = jnp.maximum(old, jnp.max(scores, axis=1, keepdims=True))
            factor = jnp.exp2((old - new) * SCALE)
            weights = jnp.exp2((scores - new) * SCALE).astype(jnp.bfloat16)
            product = jnp.dot(weights, values, preferred_element_type=jnp.float32)
            sums[rows, :] = sums[rows, :] * jnp.concatenate([factor, factor], axis=1) + product
            tops[rows, :] = new

        for s in members:

            def slot(i, carry, s=s):
                at = pl.ds(pl.multiple_of(i * BLOCK, BLOCK), BLOCK)
                block(scores_of(qa[rows, :], ka[s][at, :]), va[s][at, :])
                return carry

            lax.fori_loop(0, SLOTS, slot, 0)
        if fresh_too:
            block(fresh_scores(rows, c), nva[...])

    def fold(state, shift, rows, c, pieces, members, fresh_too):
        scaled = shift * SCALE
        summed = None if state is None else state[0][rows, :]
        for scores, values in pieces:
            scores = scores()
            wide = jnp.concatenate([scaled] * (scores.shape[1] // HD), axis=1)
            weights = jnp.exp2(scores * SCALE - wide).astype(jnp.bfloat16)
            product = jnp.dot(weights, values(), preferred_element_type=jnp.float32)
            summed = product if summed is None else summed + product
        fine = jnp.max(summed[:, HD : 2 * HD]) < HIGHEST

        @pl.when(fine)
        def _():
            state_out[0][rows, :] = summed
            if state is not state_out:
                state_out[1][rows, :] = shift

        @pl.when(jnp.logical_not(fine))
        def _():
            exact(state, shift, rows, c, members, fresh_too)

    def chunk(i, carry):
        c = i * TILE
        rows = pl.ds(pl.multiple_of(c * QR, QR), TILE * QR)
        low, high = words[c, TOKEN_CHAT], words[c + TILE - 1, TOKEN_CHAT + TOK - 1]

        def own_scores(i):
            q = queries[c + i, 0:QR, :].astype(jnp.float32)
            k = queries[c + i, QR : QR + TOK, :].astype(jnp.float32)
            k = jnp.broadcast_to(k[:, None, :], (TOK, GROUP, HD)).reshape(QR, HD)
            return jnp.broadcast_to(jnp.sum(q * k, axis=1, keepdims=True), (QR, HD))

        if first:
            shift = jnp.concatenate([own_scores(i) for i in range(TILE)], axis=0)
        else:
            shift = state_in[1][rows, :]

        def part(members, state, fresh_too):
            begins, count = [], jnp.int32(0)
            for s in members:
                begin, end = jnp.int32(0), jnp.int32(0)
                for slot in range(SLOTS):
                    chat = words[MEMBERS + s, CHAT + slot]
                    begin += (chat < low).astype(jnp.int32)
                    end += (chat <= high).astype(jnp.int32)
                begins.append(begin)
                count = jnp.maximum(count, end - begin)

            def step(slots):
                pieces = []
                for s, begin in zip(members, begins):
                    at = pl.multiple_of(jnp.minimum(begin, SLOTS - slots) * BLOCK, BLOCK)
                    at = pl.ds(at, slots * BLOCK)
                    pieces.append(
                        (
                            lambda s=s, at=at: scores_of(qa[rows, :], ka[s][at, :]),
                            lambda s=s, at=at: va[s][at, :],
                        )
                    )
                if fresh_too:
                    pieces.append((lambda: fresh_scores(rows, c), lambda: nva[...]))
                fold(state, shift, rows, c, pieces, members, fresh_too)

            under = 0
            for slots in WIDTHS:
                fits = count <= slots if under == 0 else (count > under) & (count <= slots)
                pl.when(fits)(functools.partial(step, slots))
                under = slots

        part(range(sources), state_in, last)
        return carry

    lax.fori_loop(0, MEMBERS // TILE, chunk, 0)

    if last:
        row = lax.broadcasted_iota(jnp.int32, (16, HD), 0)

        def close(c, carry):
            rows = pl.ds(pl.multiple_of(c * QR, QR), QR)
            sums = state_out[0][rows, :]
            total = jnp.maximum(sums[:, HD : 2 * HD], LOWEST)
            normal = (sums[:, 0:HD] / total).astype(jnp.bfloat16)
            logs = (state_out[1][rows, :] * SCALE + jnp.log2(total)).T
            for j in range(HEADS):
                piece = c * HEADS + j
                out[piece, 0:PIECE, :] = normal[j * PIECE : (j + 1) * PIECE, :]
                line = logs[0:16, (j // 2) * HD : (j // 2 + 1) * HD]
                top = line.astype(jnp.bfloat16).astype(jnp.float32)
                rest = line - top
                middle = rest.astype(jnp.bfloat16).astype(jnp.float32)
                low = rest - middle
                terms = jnp.where(row == 0, top, jnp.where(row == 1, middle, low))
                out[piece, PIECE:SENT, :] = terms.astype(jnp.bfloat16)
            return carry

        lax.fori_loop(0, MEMBERS, close, 0)


def attend(queries, packs, fresh, state, last=False):
    sources, first = len(packs), state is None
    operands = [queries, *packs, *fresh]
    specs = [VMEM] * (1 + sources)
    tail = pl.BlockSpec((pl.Element(3 * TOK), pl.Element(HD)), lambda i: (FRESH_K, 0))
    specs += [tail] * len(fresh)
    if not first:
        operands += state
        specs += [VMEM, VMEM]
    rows = MEMBERS * QR
    state_shapes = [(rows, 2 * HD), (rows, HD)]
    if last:
        out_shape = jax.ShapeDtypeStruct((MEMBERS * HEADS, SENT, HD), jnp.bfloat16)
    else:
        out_shape = [jax.ShapeDtypeStruct(s, jnp.float32) for s in state_shapes]
    scratch = [
        pltpu.VMEM((rows, 2 * HD), jnp.bfloat16),
        pltpu.VMEM((3 * MEMBERS, HD), jnp.int32),
        pltpu.SMEM((3 * MEMBERS, HD), jnp.int32),
        pltpu.SemaphoreType.DMA,
    ]
    scratch += [pltpu.VMEM((ROWS, 2 * HD), jnp.bfloat16)] * (2 * sources)
    if last:
        scratch += [pltpu.VMEM((BLOCK, 2 * HD), jnp.bfloat16)] * 2
        scratch += [pltpu.VMEM(s, jnp.float32) for s in state_shapes]
    return pl.pallas_call(
        functools.partial(attend_kernel, sources, first, last),
        grid=(1,),
        out_shape=out_shape,
        in_specs=specs,
        out_specs=VMEM if last else [VMEM] * 2,
        scratch_shapes=scratch,
        compiler_params=params(),
        cost_estimate=pl.CostEstimate(
            flops=sources * 4 * rows * ROWS * HD,
            bytes_accessed=sources * ROWS * HD * 4 + rows * HD * 18,
            transcendentals=sources * rows * ROWS,
        ),
        name="attend_last" if last else "attend",
    )(*operands)


def finish_kernel(place, parts, out, turned, held):
    top = None
    lines = []
    for z in range(MEMBERS):
        rows = []
        for h in range(HEADS):
            terms = parts[z * HEADS + h, PIECE:SENT, :].astype(jnp.float32)
            rows.append(terms[0:1, :] + terms[1:2, :] + terms[2:3, :])
        lines.append(rows)
    shares = [[None] * HEADS for _ in range(MEMBERS)]
    for h in range(HEADS):
        top = lines[0][h]
        for z in range(1, MEMBERS):
            top = jnp.maximum(top, lines[z][h])
        powers = [jnp.exp2(lines[z][h] - top) for z in range(MEMBERS)]
        whole = powers[0]
        for power in powers[1:]:
            whole = whole + power
        for z in range(MEMBERS):
            shares[z][h] = powers[z] / whole
    for z in range(MEMBERS):
        for h in range(HEADS):
            at = z * HEADS + h
            turned[at : at + 1, :] = shares[z][h]
    held[...] = turned[...].T
    at = pl.multiple_of(lax.rem(place[1], 2) * PIECE, PIECE)
    columns = held[pl.ds(at, PIECE), :]
    for h in range(HEADS):
        total = None
        for z in range(MEMBERS):
            i = z * HEADS + h
            term = parts[i, 0:PIECE, :].astype(jnp.float32) * columns[:, i : i + 1]
            total = term if total is None else total + term
        turned[0:PIECE, :] = total
        for g in range(GROUP):
            at = (h * GROUP + g) * HD
            out[:, at : at + HD] = turned[pl.ds(g, TOK // HEADS, stride=GROUP), :].astype(jnp.bfloat16)


def finish(place, parts):
    return pl.pallas_call(
        finish_kernel,
        out_shape=jax.ShapeDtypeStruct((TOK // HEADS, HEADS * GROUP * HD), jnp.bfloat16),
        in_specs=[SMEM, VMEM],
        out_specs=VMEM,
        scratch_shapes=[pltpu.VMEM((HD, HD), jnp.float32)] * 2,
        compiler_params=params(),
        name="finish",
    )(place, parts)


YX = ("y", "xh")
HEAD = ("xl", "core")


def up(x):
    return lax.ppermute(x, "y", [(i, (i + 1) % 4) for i in range(4)])


def down(x):
    return lax.ppermute(x, "y", [(i, (i - 1) % 4) for i in range(4)])


def across(x):
    return lax.ppermute(x, "xh", [(0, 1), (1, 0)])


def per_device(queries, cache_keys, cache_values, new_keys, new_values, block_chat, block_fill, new_chat):
    place = jnp.stack([lax.axis_index(("y", "xh", "z")), lax.axis_index(HEAD)]).astype(jnp.int32)
    mine, many = prepare(
        place,
        block_chat,
        block_fill,
        new_chat,
        queries.reshape(QR, HD),
        cache_keys[:, 0, :],
        cache_values[:, 0, :],
        new_keys[:, 0, :],
        new_values[:, 0, :],
    )
    before, after, beside = up(mine), down(mine), across(mine)
    shared = lax.all_to_all(many, "z", split_axis=0, concat_axis=0, tiled=True)
    beside_before, opposite, beside_after = up(beside), down(after), across(after)
    state = attend(shared, [mine, before, after, beside], [], None)
    far = across(opposite)
    state = attend(shared, [beside_before, opposite, beside_after], [], state)
    fresh = [mine, before, after, beside, beside_before, opposite, beside_after, far]
    parts = attend(shared, [far], fresh, state, last=True)
    parts = lax.all_to_all(parts, ("z",) + HEAD, split_axis=0, concat_axis=0, tiled=True)
    return finish(place, parts)


def solution(mesh):
    fine = Mesh(mesh.devices.reshape(4, 2, 8, 2, 2), ("y", "xh", "z", "xl", "core"))
    ctx = ("y", "xh", "z")
    rows = P(ctx, HEAD, None)
    return jax.shard_map(
        per_device,
        mesh=fine,
        in_specs=(rows,) * 5 + (P(ctx),) * 3,
        out_specs=P(ctx + HEAD, None),
        check_vma=False,
    )
```

```python
import functools
import math

import jax
import jax.numpy as jnp
from jax import lax
from jax.experimental import pallas as pl
from jax.experimental.pallas import tpu as pltpu
from jax.sharding import Mesh, PartitionSpec as P

BLOCK = 128
SLOTS = 8
ROWS = SLOTS * BLOCK
TOK = 16
GROUP = 16
HD = 128
QR = TOK * GROUP
MEMBERS = 8
HEADS = 4
FAR = -1e30
SCALE = HD**-0.5 * math.log2(math.e)
VMEM = pl.BlockSpec(memory_space=pltpu.VMEM)
SMEM = pl.BlockSpec(memory_space=pltpu.SMEM)
ANY = pl.BlockSpec(memory_space=pl.ANY)
VALUES = ROWS
FRESH_K = 2 * ROWS
FRESH_V = FRESH_K + TOK
DESC = FRESH_V + TOK
PACK = DESC + TOK
SHARED = QR + 2 * TOK
CHAT, FILL, TOKEN_CHAT, INDEX = 0, 8, 16, 32
PIECE = QR // HEADS
SENT = PIECE + 16
WIDTHS = (2, 3, 4, 6, 8)
TILE = 4
HIGHEST = 2.0**80
LOWEST = 2.0**-120


def params():
    return pltpu.CompilerParams(vmem_limit_bytes=36 * 1024 * 1024)


def prepare_kernel(place, bc, bf, nc, q, k, v, nk, nv, pack, many, sems):
    copies = [
        (k, pack.at[pl.ds(0, ROWS)]),
        (v, pack.at[pl.ds(VALUES, ROWS)]),
        (nk, pack.at[pl.ds(FRESH_K, TOK)]),
        (nv, pack.at[pl.ds(FRESH_V, TOK)]),
        (q, many.at[0, pl.ds(0, QR)]),
    ]
    started = []
    for i, (src, dst) in enumerate(copies):
        copy = pltpu.make_async_copy(src, dst, sems.at[i])
        copy.start()
        started.append(copy)
    lane = lax.broadcasted_iota(jnp.int32, (TOK, HD), 1)
    row = jnp.where(lane == INDEX, place[0], 0)
    for i in range(SLOTS):
        row = jnp.where(lane == CHAT + i, bc[i], row)
        row = jnp.where(lane == FILL + i, bf[i], row)
    for i in range(TOK):
        row = jnp.where(lane == TOKEN_CHAT + i, nc[i], row)
    desc = row.astype(jnp.float32).astype(jnp.bfloat16)
    pack[DESC:PACK, :] = desc
    for copy in started:
        copy.wait()
    own = pack[FRESH_K : FRESH_K + TOK, :]
    for i in range(MEMBERS):
        if i > 0:
            many[i, 0:QR, :] = many[0, 0:QR, :]
        many[i, QR : QR + TOK, :] = own
        many[i, QR + TOK : SHARED, :] = desc


def prepare(place, bc, bf, nc, q, k, v, nk, nv):
    return pl.pallas_call(
        prepare_kernel,
        out_shape=[
            jax.ShapeDtypeStruct((PACK, HD), jnp.bfloat16),
            jax.ShapeDtypeStruct((MEMBERS, SHARED, HD), jnp.bfloat16),
        ],
        in_specs=[SMEM] * 4 + [ANY] * 5,
        out_specs=[VMEM] * 2,
        scratch_shapes=[pltpu.SemaphoreType.DMA((5,))],
        compiler_params=pltpu.CompilerParams(vmem_limit_bytes=58 * 1024 * 1024),
        name="prepare",
    )(place, bc, bf, nc, q, k, v, nk, nv)


def scores_of(q, keys):
    return lax.dot_general(q, keys, (((1,), (1,)), ((), ())), preferred_element_type=jnp.float32)


def attend_kernel(sources, first, last, *refs):
    refs = list(refs)
    take = lambda n: [refs.pop(0) for _ in range(n)]
    queries = take(1)[0]
    packs = take(sources)
    fresh = take(MEMBERS) if last else []
    state_in = None if first else tuple(take(2))
    out = take(1)[0] if last else None
    state_out = None if last else tuple(take(2))
    qa, rows_of, words, sem = take(4)
    ka, va = take(2)
    if last:
        na, nva, sums_last, tops_last = take(4)
        state_out = (sums_last, tops_last)

    def word_row(i, tile):
        rows_of[i : i + 1, :] = tile.astype(jnp.float32).astype(jnp.int32)[0:1, :]

    for i in range(MEMBERS):
        word_row(i, queries[i, QR + TOK : SHARED, :])
    for s in range(sources):
        word_row(MEMBERS + s, packs[s][DESC:PACK, :])
    if last:
        for i in range(MEMBERS):
            word_row(2 * MEMBERS + i, fresh[i][2 * TOK : 3 * TOK, :])
    copy = pltpu.make_async_copy(rows_of, words, sem)
    copy.start()

    for s in range(sources):
        ka[s * ROWS : (s + 1) * ROWS, 0:HD] = packs[s][0:ROWS, :]
        va[s * ROWS : (s + 1) * ROWS, 0:HD] = packs[s][VALUES : VALUES + ROWS, :]
    va[:, HD : 2 * HD] = jnp.ones((sources * ROWS, HD), jnp.bfloat16)
    copy.wait()

    lane = lax.broadcasted_iota(jnp.int32, (TOK, HD), 1)
    for i in range(MEMBERS):
        qa[i * QR : (i + 1) * QR, 0:HD] = queries[i, 0:QR, :]
        for t in range(TOK):
            rows = slice(i * QR + t * GROUP, i * QR + (t + 1) * GROUP)
            hot = jnp.where(lane == words[i, TOKEN_CHAT + t], 1.0, 0.0)
            qa[rows, HD : 2 * HD] = hot.astype(jnp.bfloat16)
    lane = lax.broadcasted_iota(jnp.int32, (BLOCK, HD), 1)
    row = lax.broadcasted_iota(jnp.int32, (BLOCK, HD), 0)
    for s in range(sources):
        for slot in range(SLOTS):
            live = (lane == words[MEMBERS + s, CHAT + slot]) & (row < words[MEMBERS + s, FILL + slot])
            at = slice(s * ROWS + slot * BLOCK, s * ROWS + (slot + 1) * BLOCK)
            ka[at, HD : 2 * HD] = jnp.where(live, 0.0, FAR).astype(jnp.bfloat16)
    if last:
        lane = lax.broadcasted_iota(jnp.int32, (TOK, HD), 1)
        row = lax.broadcasted_iota(jnp.int32, (TOK, HD), 0)
        key_lane = lax.broadcasted_iota(jnp.int32, (1, HD), 1)
        key_pos = jnp.zeros((1, HD), jnp.int32)
        for i in range(MEMBERS):
            at = slice(i * TOK, (i + 1) * TOK)
            na[at, 0:HD] = fresh[i][0:TOK, :]
            nva[at, 0:HD] = fresh[i][TOK : 2 * TOK, :]
            chat = jnp.zeros((TOK, HD), jnp.int32)
            for t in range(TOK):
                chat = jnp.where(row == t, words[2 * MEMBERS + i, TOKEN_CHAT + t], chat)
            na[at, HD : 2 * HD] = jnp.where(lane == chat, 0.0, FAR).astype(jnp.bfloat16)
            start = words[2 * MEMBERS + i, INDEX] * TOK
            key_pos = jnp.where(key_lane // TOK == i, start + key_lane % TOK, key_pos)
        nva[:, HD : 2 * HD] = jnp.ones((BLOCK, HD), jnp.bfloat16)

    def fresh_scores(rows, c):
        token = lax.broadcasted_iota(jnp.int32, (TILE * QR, HD), 0) // GROUP
        seen = key_pos <= words[c, INDEX] * TOK + token
        return jnp.where(seen, scores_of(qa[rows, :], na[...]), FAR)

    def exact(rows, c):
        sums, tops = state_out
        if first:
            sums[rows, :] = jnp.zeros((TILE * QR, 2 * HD), jnp.float32)
        else:
            sums[rows, :] = state_in[0][rows, :]

        def block(scores, values):
            old = tops[rows, :]
            new = jnp.maximum(old, jnp.max(scores, axis=1, keepdims=True))
            factor = jnp.exp2((old - new) * SCALE)
            weights = jnp.exp2((scores - new) * SCALE).astype(jnp.bfloat16)
            product = jnp.dot(weights, values, preferred_element_type=jnp.float32)
            sums[rows, :] = sums[rows, :] * jnp.concatenate([factor, factor], axis=1) + product
            tops[rows, :] = new

        def slot(i, carry):
            at = pl.ds(pl.multiple_of(i * BLOCK, BLOCK), BLOCK)
            block(scores_of(qa[rows, :], ka[at, :]), va[at, :])
            return carry

        lax.fori_loop(0, sources * SLOTS, slot, 0)
        if last:
            block(fresh_scores(rows, c), nva[...])

    def chunk(i, carry):
        c = i * TILE
        rows = pl.ds(pl.multiple_of(c * QR, QR), TILE * QR)
        low, high = words[c, TOKEN_CHAT], words[c + TILE - 1, TOKEN_CHAT + TOK - 1]

        def own_scores(i):
            q = queries[c + i, 0:QR, :].astype(jnp.float32)
            k = queries[c + i, QR : QR + TOK, :].astype(jnp.float32)
            k = jnp.broadcast_to(k[:, None, :], (TOK, GROUP, HD)).reshape(QR, HD)
            return jnp.broadcast_to(jnp.sum(q * k, axis=1, keepdims=True), (QR, HD))

        sums, tops = state_out
        if first:
            tops[rows, :] = jnp.concatenate([own_scores(i) for i in range(TILE)], axis=0)
            sums[rows, :] = jnp.zeros((TILE * QR, 2 * HD), jnp.float32)
        else:
            tops[rows, :] = state_in[1][rows, :]
            sums[rows, :] = state_in[0][rows, :]

        def add(scores, values):
            shift = tops[rows, :] * SCALE
            wide = jnp.concatenate([shift] * (scores.shape[1] // HD), axis=1)
            weights = jnp.exp2(scores * SCALE - wide).astype(jnp.bfloat16)
            sums[rows, :] += jnp.dot(weights, values, preferred_element_type=jnp.float32)

        def source(s, carry):
            begin, end = jnp.int32(0), jnp.int32(0)
            for slot in range(SLOTS):
                chat = words[MEMBERS + s, CHAT + slot]
                begin += (chat < low).astype(jnp.int32)
                end += (chat <= high).astype(jnp.int32)
            count = end - begin

            def some(slots):
                start = s * SLOTS + jnp.minimum(begin, SLOTS - slots)
                at = pl.ds(pl.multiple_of(start * BLOCK, BLOCK), slots * BLOCK)
                add(scores_of(qa[rows, :], ka[at, :]), va[at, :])

            under = 0
            for slots in WIDTHS:
                pl.when((count > under) & (count <= slots))(functools.partial(some, slots))
                under = slots
            return carry

        lax.fori_loop(0, sources, source, 0)
        if last:
            add(fresh_scores(rows, c), nva[...])
        fine = jnp.max(sums[rows, HD : 2 * HD]) < HIGHEST

        @pl.when(jnp.logical_not(fine))
        def _():
            exact(rows, c)

        return carry

    lax.fori_loop(0, MEMBERS // TILE, chunk, 0)

    if last:
        row = lax.broadcasted_iota(jnp.int32, (16, HD), 0)

        def close(c, carry):
            rows = pl.ds(pl.multiple_of(c * QR, QR), QR)
            sums = state_out[0][rows, :]
            total = jnp.maximum(sums[:, HD : 2 * HD], LOWEST)
            normal = (sums[:, 0:HD] / total).astype(jnp.bfloat16)
            logs = (state_out[1][rows, :] * SCALE + jnp.log2(total)).T
            for j in range(HEADS):
                piece = c * HEADS + j
                out[piece, 0:PIECE, :] = normal[j * PIECE : (j + 1) * PIECE, :]
                line = logs[0:16, (j // 2) * HD : (j // 2 + 1) * HD]
                top = line.astype(jnp.bfloat16).astype(jnp.float32)
                rest = line - top
                middle = rest.astype(jnp.bfloat16).astype(jnp.float32)
                low = rest - middle
                terms = jnp.where(row == 0, top, jnp.where(row == 1, middle, low))
                out[piece, PIECE:SENT, :] = terms.astype(jnp.bfloat16)
            return carry

        lax.fori_loop(0, MEMBERS, close, 0)


def attend(queries, packs, fresh, state, last=False):
    sources, first = len(packs), state is None
    operands = [queries, *packs, *fresh]
    specs = [VMEM] * (1 + sources)
    tail = pl.BlockSpec((pl.Element(3 * TOK), pl.Element(HD)), lambda i: (FRESH_K, 0))
    specs += [tail] * len(fresh)
    if not first:
        operands += state
        specs += [VMEM, VMEM]
    rows = MEMBERS * QR
    state_shapes = [(rows, 2 * HD), (rows, HD)]
    if last:
        out_shape = jax.ShapeDtypeStruct((MEMBERS * HEADS, SENT, HD), jnp.bfloat16)
    else:
        out_shape = [jax.ShapeDtypeStruct(s, jnp.float32) for s in state_shapes]
    scratch = [
        pltpu.VMEM((rows, 2 * HD), jnp.bfloat16),
        pltpu.VMEM((3 * MEMBERS, HD), jnp.int32),
        pltpu.SMEM((3 * MEMBERS, HD), jnp.int32),
        pltpu.SemaphoreType.DMA,
    ]
    scratch += [pltpu.VMEM((sources * ROWS, 2 * HD), jnp.bfloat16)] * 2
    if last:
        scratch += [pltpu.VMEM((BLOCK, 2 * HD), jnp.bfloat16)] * 2
        scratch += [pltpu.VMEM(s, jnp.float32) for s in state_shapes]
    return pl.pallas_call(
        functools.partial(attend_kernel, sources, first, last),
        grid=(1,),
        out_shape=out_shape,
        in_specs=specs,
        out_specs=VMEM if last else [VMEM] * 2,
        scratch_shapes=scratch,
        compiler_params=params(),
        cost_estimate=pl.CostEstimate(
            flops=sources * 4 * rows * ROWS * HD,
            bytes_accessed=sources * ROWS * HD * 4 + rows * HD * 18,
            transcendentals=sources * rows * ROWS,
        ),
        name="attend_last" if last else "attend",
    )(*operands)


def finish_kernel(place, parts, out, turned, held):
    top = None
    lines = []
    for z in range(MEMBERS):
        rows = []
        for h in range(HEADS):
            terms = parts[z * HEADS + h, PIECE:SENT, :].astype(jnp.float32)
            rows.append(terms[0:1, :] + terms[1:2, :] + terms[2:3, :])
        lines.append(rows)
    shares = [[None] * HEADS for _ in range(MEMBERS)]
    for h in range(HEADS):
        top = lines[0][h]
        for z in range(1, MEMBERS):
            top = jnp.maximum(top, lines[z][h])
        powers = [jnp.exp2(lines[z][h] - top) for z in range(MEMBERS)]
        whole = powers[0]
        for power in powers[1:]:
            whole = whole + power
        for z in range(MEMBERS):
            shares[z][h] = powers[z] / whole
    for z in range(MEMBERS):
        for h in range(HEADS):
            at = z * HEADS + h
            turned[at : at + 1, :] = shares[z][h]
    held[...] = turned[...].T
    at = pl.multiple_of(lax.rem(place[1], 2) * PIECE, PIECE)
    columns = held[pl.ds(at, PIECE), :]
    for h in range(HEADS):
        total = None
        for z in range(MEMBERS):
            i = z * HEADS + h
            term = parts[i, 0:PIECE, :].astype(jnp.float32) * columns[:, i : i + 1]
            total = term if total is None else total + term
        turned[0:PIECE, :] = total
        for g in range(GROUP):
            at = (h * GROUP + g) * HD
            out[:, at : at + HD] = turned[pl.ds(g, TOK // HEADS, stride=GROUP), :].astype(jnp.bfloat16)


def finish(place, parts):
    return pl.pallas_call(
        finish_kernel,
        out_shape=jax.ShapeDtypeStruct((TOK // HEADS, HEADS * GROUP * HD), jnp.bfloat16),
        in_specs=[SMEM, VMEM],
        out_specs=VMEM,
        scratch_shapes=[pltpu.VMEM((HD, HD), jnp.float32)] * 2,
        compiler_params=params(),
        name="finish",
    )(place, parts)


YX = ("y", "xh")
HEAD = ("xl", "core")


def up(x):
    return lax.ppermute(x, "y", [(i, (i + 1) % 4) for i in range(4)])


def down(x):
    return lax.ppermute(x, "y", [(i, (i - 1) % 4) for i in range(4)])


def across(x):
    return lax.ppermute(x, "xh", [(0, 1), (1, 0)])


def per_device(queries, cache_keys, cache_values, new_keys, new_values, block_chat, block_fill, new_chat):
    place = jnp.stack([lax.axis_index(("y", "xh", "z")), lax.axis_index(HEAD)]).astype(jnp.int32)
    mine, many = prepare(
        place,
        block_chat,
        block_fill,
        new_chat,
        queries.reshape(QR, HD),
        cache_keys[:, 0, :],
        cache_values[:, 0, :],
        new_keys[:, 0, :],
        new_values[:, 0, :],
    )
    before, after, beside = up(mine), down(mine), across(mine)
    shared = lax.all_to_all(many, "z", split_axis=0, concat_axis=0, tiled=True)
    beside_before, opposite, beside_after = up(beside), down(after), across(after)
    state = attend(shared, [mine, before, after, beside], [], None)
    far = across(opposite)
    state = attend(shared, [beside_before, opposite, beside_after], [], state)
    fresh = [mine, before, after, beside, beside_before, opposite, beside_after, far]
    parts = attend(shared, [far], fresh, state, last=True)
    parts = lax.all_to_all(parts, ("z",) + HEAD, split_axis=0, concat_axis=0, tiled=True)
    return finish(place, parts)


def solution(mesh):
    fine = Mesh(mesh.devices.reshape(4, 2, 8, 2, 2), ("y", "xh", "z", "xl", "core"))
    ctx = ("y", "xh", "z")
    rows = P(ctx, HEAD, None)
    return jax.shard_map(
        per_device,
        mesh=fine,
        in_specs=(rows,) * 5 + (P(ctx),) * 3,
        out_specs=P(ctx + HEAD, None),
        check_vma=False,
    )
```

```python
import functools
import math

import jax
import jax.numpy as jnp
from jax import lax
from jax.experimental import pallas as pl
from jax.experimental.pallas import tpu as pltpu
from jax.sharding import Mesh, PartitionSpec as P

BLOCK = 128
SLOTS = 8
ROWS = SLOTS * BLOCK
TOK = 16
GROUP = 16
HD = 128
QR = TOK * GROUP
MEMBERS = 8
HEADS = 4
FAR = -1e30
SCALE = HD**-0.5 * math.log2(math.e)
VMEM = pl.BlockSpec(memory_space=pltpu.VMEM)
SMEM = pl.BlockSpec(memory_space=pltpu.SMEM)
ANY = pl.BlockSpec(memory_space=pl.ANY)
VALUES = ROWS
FRESH_K = 2 * ROWS
FRESH_V = FRESH_K + TOK
DESC = FRESH_V + TOK
PACK = DESC + TOK
SHARED = QR + 2 * TOK
CHAT, FILL, TOKEN_CHAT, INDEX = 0, 8, 16, 32
PIECE = QR // HEADS
SENT = PIECE + 16
WIDTHS = (2, 3, 4, 6, 8)
TILE = 4
HIGHEST = 2.0**80
LOWEST = 2.0**-120


def params():
    return pltpu.CompilerParams(vmem_limit_bytes=36 * 1024 * 1024)


def prepare_kernel(place, bc, bf, nc, q, k, v, nk, nv, pack, many, sems):
    copies = [
        (k, pack.at[pl.ds(0, ROWS)]),
        (v, pack.at[pl.ds(VALUES, ROWS)]),
        (nk, pack.at[pl.ds(FRESH_K, TOK)]),
        (nv, pack.at[pl.ds(FRESH_V, TOK)]),
        (q, many.at[0, pl.ds(0, QR)]),
    ]
    started = []
    for i, (src, dst) in enumerate(copies):
        copy = pltpu.make_async_copy(src, dst, sems.at[i])
        copy.start()
        started.append(copy)
    lane = lax.broadcasted_iota(jnp.int32, (TOK, HD), 1)
    row = jnp.where(lane == INDEX, place[0], 0)
    for i in range(SLOTS):
        row = jnp.where(lane == CHAT + i, bc[i], row)
        row = jnp.where(lane == FILL + i, bf[i], row)
    for i in range(TOK):
        row = jnp.where(lane == TOKEN_CHAT + i, nc[i], row)
    desc = row.astype(jnp.float32).astype(jnp.bfloat16)
    pack[DESC:PACK, :] = desc
    for copy in started:
        copy.wait()
    own = pack[FRESH_K : FRESH_K + TOK, :]
    for i in range(MEMBERS):
        if i > 0:
            many[i, 0:QR, :] = many[0, 0:QR, :]
        many[i, QR : QR + TOK, :] = own
        many[i, QR + TOK : SHARED, :] = desc


def prepare(place, bc, bf, nc, q, k, v, nk, nv):
    return pl.pallas_call(
        prepare_kernel,
        out_shape=[
            jax.ShapeDtypeStruct((PACK, HD), jnp.bfloat16),
            jax.ShapeDtypeStruct((MEMBERS, SHARED, HD), jnp.bfloat16),
        ],
        in_specs=[SMEM] * 4 + [ANY] * 5,
        out_specs=[VMEM] * 2,
        scratch_shapes=[pltpu.SemaphoreType.DMA((5,))],
        compiler_params=pltpu.CompilerParams(vmem_limit_bytes=58 * 1024 * 1024),
        name="prepare",
    )(place, bc, bf, nc, q, k, v, nk, nv)


def scores_of(q, keys):
    return lax.dot_general(q, keys, (((1,), (1,)), ((), ())), preferred_element_type=jnp.float32)


def attend_kernel(sources, first, last, *refs):
    refs = list(refs)
    take = lambda n: [refs.pop(0) for _ in range(n)]
    queries = take(1)[0]
    packs = take(sources)
    fresh = take(MEMBERS) if last else []
    state_in = None if first else tuple(take(2))
    out = take(1)[0] if last else None
    state_out = None if last else tuple(take(2))
    qa, rows_of, words, sem = take(4)
    ka, va = take(2)
    if last:
        na, nva, sums_last, tops_last = take(4)
        state_out = (sums_last, tops_last)

    def word_row(i, tile):
        rows_of[i : i + 1, :] = tile.astype(jnp.float32).astype(jnp.int32)[0:1, :]

    for i in range(MEMBERS):
        word_row(i, queries[i, QR + TOK : SHARED, :])
    for s in range(sources):
        word_row(MEMBERS + s, packs[s][DESC:PACK, :])
    if last:
        for i in range(MEMBERS):
            word_row(2 * MEMBERS + i, fresh[i][2 * TOK : 3 * TOK, :])
    copy = pltpu.make_async_copy(rows_of, words, sem)
    copy.start()

    for s in range(sources):
        ka[s * ROWS : (s + 1) * ROWS, 0:HD] = packs[s][0:ROWS, :]
        va[s * ROWS : (s + 1) * ROWS, 0:HD] = packs[s][VALUES : VALUES + ROWS, :]
    va[:, HD : 2 * HD] = jnp.ones((sources * ROWS, HD), jnp.bfloat16)
    copy.wait()

    lane = lax.broadcasted_iota(jnp.int32, (TOK, HD), 1)
    for i in range(MEMBERS):
        qa[i * QR : (i + 1) * QR, 0:HD] = queries[i, 0:QR, :]
        for t in range(TOK):
            rows = slice(i * QR + t * GROUP, i * QR + (t + 1) * GROUP)
            hot = jnp.where(lane == words[i, TOKEN_CHAT + t], 1.0, 0.0)
            qa[rows, HD : 2 * HD] = hot.astype(jnp.bfloat16)
    lane = lax.broadcasted_iota(jnp.int32, (BLOCK, HD), 1)
    row = lax.broadcasted_iota(jnp.int32, (BLOCK, HD), 0)
    for s in range(sources):
        for slot in range(SLOTS):
            live = (lane == words[MEMBERS + s, CHAT + slot]) & (row < words[MEMBERS + s, FILL + slot])
            at = slice(s * ROWS + slot * BLOCK, s * ROWS + (slot + 1) * BLOCK)
            ka[at, HD : 2 * HD] = jnp.where(live, 0.0, FAR).astype(jnp.bfloat16)
    if last:
        lane = lax.broadcasted_iota(jnp.int32, (TOK, HD), 1)
        row = lax.broadcasted_iota(jnp.int32, (TOK, HD), 0)
        key_lane = lax.broadcasted_iota(jnp.int32, (1, HD), 1)
        key_pos = jnp.zeros((1, HD), jnp.int32)
        for i in range(MEMBERS):
            at = slice(i * TOK, (i + 1) * TOK)
            na[at, 0:HD] = fresh[i][0:TOK, :]
            nva[at, 0:HD] = fresh[i][TOK : 2 * TOK, :]
            chat = jnp.zeros((TOK, HD), jnp.int32)
            for t in range(TOK):
                chat = jnp.where(row == t, words[2 * MEMBERS + i, TOKEN_CHAT + t], chat)
            na[at, HD : 2 * HD] = jnp.where(lane == chat, 0.0, FAR).astype(jnp.bfloat16)
            start = words[2 * MEMBERS + i, INDEX] * TOK
            key_pos = jnp.where(key_lane // TOK == i, start + key_lane % TOK, key_pos)
        nva[:, HD : 2 * HD] = jnp.ones((BLOCK, HD), jnp.bfloat16)

    def fresh_scores(rows, c):
        token = lax.broadcasted_iota(jnp.int32, (TILE * QR, HD), 0) // GROUP
        seen = key_pos <= words[c, INDEX] * TOK + token
        return jnp.where(seen, scores_of(qa[rows, :], na[...]), FAR)

    def exact(rows, c):
        sums, tops = state_out
        if first:
            sums[rows, :] = jnp.zeros((TILE * QR, 2 * HD), jnp.float32)
        else:
            sums[rows, :] = state_in[0][rows, :]

        def block(scores, values):
            old = tops[rows, :]
            new = jnp.maximum(old, jnp.max(scores, axis=1, keepdims=True))
            factor = jnp.exp2((old - new) * SCALE)
            weights = jnp.exp2((scores - new) * SCALE).astype(jnp.bfloat16)
            product = jnp.dot(weights, values, preferred_element_type=jnp.float32)
            sums[rows, :] = sums[rows, :] * jnp.concatenate([factor, factor], axis=1) + product
            tops[rows, :] = new

        def slot(i, carry):
            at = pl.ds(pl.multiple_of(i * BLOCK, BLOCK), BLOCK)
            block(scores_of(qa[rows, :], ka[at, :]), va[at, :])
            return carry

        lax.fori_loop(0, sources * SLOTS, slot, 0)
        if last:
            block(fresh_scores(rows, c), nva[...])

    def chunk(i, carry):
        c = i * TILE
        rows = pl.ds(pl.multiple_of(c * QR, QR), TILE * QR)
        low, high = words[c, TOKEN_CHAT], words[c + TILE - 1, TOKEN_CHAT + TOK - 1]

        def own_scores(i):
            q = queries[c + i, 0:QR, :].astype(jnp.float32)
            k = queries[c + i, QR : QR + TOK, :].astype(jnp.float32)
            k = jnp.broadcast_to(k[:, None, :], (TOK, GROUP, HD)).reshape(QR, HD)
            return jnp.broadcast_to(jnp.sum(q * k, axis=1, keepdims=True), (QR, HD))

        sums, tops = state_out
        if first:
            tops[rows, :] = jnp.concatenate([own_scores(i) for i in range(TILE)], axis=0)
            sums[rows, :] = jnp.zeros((TILE * QR, 2 * HD), jnp.float32)
        else:
            tops[rows, :] = state_in[1][rows, :]
            sums[rows, :] = state_in[0][rows, :]

        def add(scores, values):
            shift = tops[rows, :] * SCALE
            wide = jnp.concatenate([shift] * (scores.shape[1] // HD), axis=1)
            weights = jnp.exp2(scores * SCALE - wide).astype(jnp.bfloat16)
            sums[rows, :] += jnp.dot(weights, values, preferred_element_type=jnp.float32)

        def source(s, carry):
            begin, end = jnp.int32(0), jnp.int32(0)
            for slot in range(SLOTS):
                chat = words[MEMBERS + s, CHAT + slot]
                begin += (chat < low).astype(jnp.int32)
                end += (chat <= high).astype(jnp.int32)
            count = end - begin

            def some(slots):
                start = s * SLOTS + jnp.minimum(begin, SLOTS - slots)
                at = pl.ds(pl.multiple_of(start * BLOCK, BLOCK), slots * BLOCK)
                add(scores_of(qa[rows, :], ka[at, :]), va[at, :])

            under = 0
            for slots in WIDTHS:
                pl.when((count > under) & (count <= slots))(functools.partial(some, slots))
                under = slots
            return carry

        lax.fori_loop(0, sources, source, 0)
        if last:
            add(fresh_scores(rows, c), nva[...])
        fine = jnp.max(sums[rows, HD : 2 * HD]) < HIGHEST

        @pl.when(jnp.logical_not(fine))
        def _():
            exact(rows, c)

        return carry

    lax.fori_loop(0, MEMBERS // TILE, chunk, 0)

    if last:
        row = lax.broadcasted_iota(jnp.int32, (16, HD), 0)

        def close(c, carry):
            rows = pl.ds(pl.multiple_of(c * QR, QR), QR)
            sums = state_out[0][rows, :]
            total = jnp.maximum(sums[:, HD : 2 * HD], LOWEST)
            normal = (sums[:, 0:HD] / total).astype(jnp.bfloat16)
            logs = (state_out[1][rows, :] * SCALE + jnp.log2(total)).T
            for j in range(HEADS):
                piece = c * HEADS + j
                out[piece, 0:PIECE, :] = normal[j * PIECE : (j + 1) * PIECE, :]
                line = logs[0:16, (j // 2) * HD : (j // 2 + 1) * HD]
                top = line.astype(jnp.bfloat16).astype(jnp.float32)
                rest = line - top
                middle = rest.astype(jnp.bfloat16).astype(jnp.float32)
                low = rest - middle
                terms = jnp.where(row == 0, top, jnp.where(row == 1, middle, low))
                out[piece, PIECE:SENT, :] = terms.astype(jnp.bfloat16)
            return carry

        lax.fori_loop(0, MEMBERS, close, 0)


def attend(queries, packs, fresh, state, last=False):
    sources, first = len(packs), state is None
    operands = [queries, *packs, *fresh]
    specs = [VMEM] * (1 + sources)
    tail = pl.BlockSpec((pl.Element(3 * TOK), pl.Element(HD)), lambda i: (FRESH_K, 0))
    specs += [tail] * len(fresh)
    if not first:
        operands += state
        specs += [VMEM, VMEM]
    rows = MEMBERS * QR
    state_shapes = [(rows, 2 * HD), (rows, HD)]
    if last:
        out_shape = jax.ShapeDtypeStruct((MEMBERS * HEADS, SENT, HD), jnp.bfloat16)
    else:
        out_shape = [jax.ShapeDtypeStruct(s, jnp.float32) for s in state_shapes]
    scratch = [
        pltpu.VMEM((rows, 2 * HD), jnp.bfloat16),
        pltpu.VMEM((3 * MEMBERS, HD), jnp.int32),
        pltpu.SMEM((3 * MEMBERS, HD), jnp.int32),
        pltpu.SemaphoreType.DMA,
    ]
    scratch += [pltpu.VMEM((sources * ROWS, 2 * HD), jnp.bfloat16)] * 2
    if last:
        scratch += [pltpu.VMEM((BLOCK, 2 * HD), jnp.bfloat16)] * 2
        scratch += [pltpu.VMEM(s, jnp.float32) for s in state_shapes]
    return pl.pallas_call(
        functools.partial(attend_kernel, sources, first, last),
        grid=(1,),
        out_shape=out_shape,
        in_specs=specs,
        out_specs=VMEM if last else [VMEM] * 2,
        scratch_shapes=scratch,
        compiler_params=params(),
        cost_estimate=pl.CostEstimate(
            flops=sources * 4 * rows * ROWS * HD,
            bytes_accessed=sources * ROWS * HD * 4 + rows * HD * 18,
            transcendentals=sources * rows * ROWS,
        ),
        name="attend_last" if last else "attend",
    )(*operands)


def finish_kernel(place, parts, out, turned, held):
    top = None
    lines = []
    for z in range(MEMBERS):
        rows = []
        for h in range(HEADS):
            terms = parts[z * HEADS + h, PIECE:SENT, :].astype(jnp.float32)
            rows.append(terms[0:1, :] + terms[1:2, :] + terms[2:3, :])
        lines.append(rows)
    shares = [[None] * HEADS for _ in range(MEMBERS)]
    for h in range(HEADS):
        top = lines[0][h]
        for z in range(1, MEMBERS):
            top = jnp.maximum(top, lines[z][h])
        powers = [jnp.exp2(lines[z][h] - top) for z in range(MEMBERS)]
        whole = powers[0]
        for power in powers[1:]:
            whole = whole + power
        for z in range(MEMBERS):
            shares[z][h] = powers[z] / whole
    for z in range(MEMBERS):
        for h in range(HEADS):
            at = z * HEADS + h
            turned[at : at + 1, :] = shares[z][h]
    held[...] = turned[...].T
    at = pl.multiple_of(lax.rem(place[1], 2) * PIECE, PIECE)
    columns = held[pl.ds(at, PIECE), :]
    for h in range(HEADS):
        total = None
        for z in range(MEMBERS):
            i = z * HEADS + h
            term = parts[i, 0:PIECE, :].astype(jnp.float32) * columns[:, i : i + 1]
            total = term if total is None else total + term
        turned[0:PIECE, :] = total
        for g in range(GROUP):
            at = (h * GROUP + g) * HD
            out[:, at : at + HD] = turned[pl.ds(g, TOK // HEADS, stride=GROUP), :].astype(jnp.bfloat16)


def finish(place, parts):
    return pl.pallas_call(
        finish_kernel,
        out_shape=jax.ShapeDtypeStruct((TOK // HEADS, HEADS * GROUP * HD), jnp.bfloat16),
        in_specs=[SMEM, VMEM],
        out_specs=VMEM,
        scratch_shapes=[pltpu.VMEM((HD, HD), jnp.float32)] * 2,
        compiler_params=params(),
        name="finish",
    )(place, parts)


YX = ("y", "xh")
HEAD = ("xl", "core")


def up(x):
    return lax.ppermute(x, "y", [(i, (i + 1) % 4) for i in range(4)])


def down(x):
    return lax.ppermute(x, "y", [(i, (i - 1) % 4) for i in range(4)])


def across(x):
    return lax.ppermute(x, "xh", [(0, 1), (1, 0)])


def per_device(queries, cache_keys, cache_values, new_keys, new_values, block_chat, block_fill, new_chat):
    place = jnp.stack([lax.axis_index(("y", "xh", "z")), lax.axis_index(HEAD)]).astype(jnp.int32)
    mine, many = prepare(
        place,
        block_chat,
        block_fill,
        new_chat,
        queries.reshape(QR, HD),
        cache_keys[:, 0, :],
        cache_values[:, 0, :],
        new_keys[:, 0, :],
        new_values[:, 0, :],
    )
    before, after, beside = up(mine), down(mine), across(mine)
    shared = lax.all_to_all(many, "z", split_axis=0, concat_axis=0, tiled=True)
    beside_before, opposite, beside_after = up(beside), down(after), across(after)
    far = across(opposite)
    near = [mine, after, beside, before, opposite, beside_after]
    state = attend(shared, near, [], None)
    fresh = [mine, before, after, beside, beside_before, opposite, beside_after, far]
    parts = attend(shared, [beside_before, far], fresh, state, last=True)
    parts = lax.all_to_all(parts, ("z",) + HEAD, split_axis=0, concat_axis=0, tiled=True)
    return finish(place, parts)


def solution(mesh):
    fine = Mesh(mesh.devices.reshape(4, 2, 8, 2, 2), ("y", "xh", "z", "xl", "core"))
    ctx = ("y", "xh", "z")
    rows = P(ctx, HEAD, None)
    return jax.shard_map(
        per_device,
        mesh=fine,
        in_specs=(rows,) * 5 + (P(ctx),) * 3,
        out_specs=P(ctx + HEAD, None),
        check_vma=False,
    )
```

```python
import functools
import math

import jax
import jax.numpy as jnp
from jax import lax
from jax.experimental import pallas as pl
from jax.experimental.pallas import tpu as pltpu
from jax.sharding import Mesh, PartitionSpec as P

BLOCK = 128
SLOTS = 8
ROWS = SLOTS * BLOCK
TOK = 16
GROUP = 16
HD = 128
QR = TOK * GROUP
MEMBERS = 8
HEADS = 4
FAR = -1e30
SCALE = HD**-0.5 * math.log2(math.e)
VMEM = pl.BlockSpec(memory_space=pltpu.VMEM)
SMEM = pl.BlockSpec(memory_space=pltpu.SMEM)
ANY = pl.BlockSpec(memory_space=pl.ANY)
VALUES = ROWS
FRESH_K = 2 * ROWS
FRESH_V = FRESH_K + TOK
DESC = FRESH_V + TOK
PACK = DESC + TOK
SHARED = QR + 2 * TOK
CHAT, FILL, TOKEN_CHAT, INDEX = 0, 8, 16, 32
PIECE = QR // HEADS
SENT = PIECE + 16
WIDTHS = (2, 3, 4, 6, 8)
TILE = 4
HIGHEST = 2.0**80
LOWEST = 2.0**-120


def params():
    return pltpu.CompilerParams(vmem_limit_bytes=36 * 1024 * 1024)


def prepare_kernel(place, bc, bf, nc, q, k, v, nk, nv, pack, many, sems):
    copies = [
        (k, pack.at[pl.ds(0, ROWS)]),
        (v, pack.at[pl.ds(VALUES, ROWS)]),
        (nk, pack.at[pl.ds(FRESH_K, TOK)]),
        (nv, pack.at[pl.ds(FRESH_V, TOK)]),
        (q, many.at[0, pl.ds(0, QR)]),
    ]
    started = []
    for i, (src, dst) in enumerate(copies):
        copy = pltpu.make_async_copy(src, dst, sems.at[i])
        copy.start()
        started.append(copy)
    lane = lax.broadcasted_iota(jnp.int32, (TOK, HD), 1)
    row = jnp.where(lane == INDEX, place[0], 0)
    for i in range(SLOTS):
        row = jnp.where(lane == CHAT + i, bc[i], row)
        row = jnp.where(lane == FILL + i, bf[i], row)
    for i in range(TOK):
        row = jnp.where(lane == TOKEN_CHAT + i, nc[i], row)
    desc = row.astype(jnp.float32).astype(jnp.bfloat16)
    pack[DESC:PACK, :] = desc
    for copy in started:
        copy.wait()
    own = pack[FRESH_K : FRESH_K + TOK, :]
    for i in range(MEMBERS):
        if i > 0:
            many[i, 0:QR, :] = many[0, 0:QR, :]
        many[i, QR : QR + TOK, :] = own
        many[i, QR + TOK : SHARED, :] = desc


def prepare(place, bc, bf, nc, q, k, v, nk, nv):
    return pl.pallas_call(
        prepare_kernel,
        out_shape=[
            jax.ShapeDtypeStruct((PACK, HD), jnp.bfloat16),
            jax.ShapeDtypeStruct((MEMBERS, SHARED, HD), jnp.bfloat16),
        ],
        in_specs=[SMEM] * 4 + [ANY] * 5,
        out_specs=[VMEM] * 2,
        scratch_shapes=[pltpu.SemaphoreType.DMA((5,))],
        compiler_params=pltpu.CompilerParams(vmem_limit_bytes=58 * 1024 * 1024),
        name="prepare",
    )(place, bc, bf, nc, q, k, v, nk, nv)


def scores_of(q, keys):
    return lax.dot_general(q, keys, (((1,), (1,)), ((), ())), preferred_element_type=jnp.float32)


def attend_kernel(sources, first, last, *refs):
    refs = list(refs)
    take = lambda n: [refs.pop(0) for _ in range(n)]
    queries = take(1)[0]
    packs = take(sources)
    fresh = take(MEMBERS) if last else []
    state_in = None if first else tuple(take(2))
    out = take(1)[0] if last else None
    state_out = None if last else tuple(take(2))
    qa, rows_of, words, sem = take(4)
    ka, va = take(2)
    if last:
        na, nva, sums_last, tops_last = take(4)
        state_out = (sums_last, tops_last)

    def word_row(i, tile):
        rows_of[i : i + 1, :] = tile.astype(jnp.float32).astype(jnp.int32)[0:1, :]

    for i in range(MEMBERS):
        word_row(i, queries[i, QR + TOK : SHARED, :])
    for s in range(sources):
        word_row(MEMBERS + s, packs[s][DESC:PACK, :])
    if last:
        for i in range(MEMBERS):
            word_row(2 * MEMBERS + i, fresh[i][2 * TOK : 3 * TOK, :])
    copy = pltpu.make_async_copy(rows_of, words, sem)
    copy.start()

    for s in range(sources):
        ka[s * ROWS : (s + 1) * ROWS, 0:HD] = packs[s][0:ROWS, :]
        va[s * ROWS : (s + 1) * ROWS, 0:HD] = packs[s][VALUES : VALUES + ROWS, :]
    va[:, HD : 2 * HD] = jnp.ones((sources * ROWS, HD), jnp.bfloat16)
    copy.wait()

    lane = lax.broadcasted_iota(jnp.int32, (TOK, HD), 1)
    for i in range(MEMBERS):
        qa[i * QR : (i + 1) * QR, 0:HD] = queries[i, 0:QR, :]
        for t in range(TOK):
            rows = slice(i * QR + t * GROUP, i * QR + (t + 1) * GROUP)
            hot = jnp.where(lane == words[i, TOKEN_CHAT + t], 1.0, 0.0)
            qa[rows, HD : 2 * HD] = hot.astype(jnp.bfloat16)
    lane = lax.broadcasted_iota(jnp.int32, (BLOCK, HD), 1)
    row = lax.broadcasted_iota(jnp.int32, (BLOCK, HD), 0)
    for s in range(sources):
        for slot in range(SLOTS):
            live = (lane == words[MEMBERS + s, CHAT + slot]) & (row < words[MEMBERS + s, FILL + slot])
            at = slice(s * ROWS + slot * BLOCK, s * ROWS + (slot + 1) * BLOCK)
            ka[at, HD : 2 * HD] = jnp.where(live, 0.0, FAR).astype(jnp.bfloat16)
    if last:
        lane = lax.broadcasted_iota(jnp.int32, (TOK, HD), 1)
        row = lax.broadcasted_iota(jnp.int32, (TOK, HD), 0)
        key_lane = lax.broadcasted_iota(jnp.int32, (1, HD), 1)
        key_pos = jnp.zeros((1, HD), jnp.int32)
        for i in range(MEMBERS):
            at = slice(i * TOK, (i + 1) * TOK)
            na[at, 0:HD] = fresh[i][0:TOK, :]
            nva[at, 0:HD] = fresh[i][TOK : 2 * TOK, :]
            chat = jnp.zeros((TOK, HD), jnp.int32)
            for t in range(TOK):
                chat = jnp.where(row == t, words[2 * MEMBERS + i, TOKEN_CHAT + t], chat)
            na[at, HD : 2 * HD] = jnp.where(lane == chat, 0.0, FAR).astype(jnp.bfloat16)
            start = words[2 * MEMBERS + i, INDEX] * TOK
            key_pos = jnp.where(key_lane // TOK == i, start + key_lane % TOK, key_pos)
        nva[:, HD : 2 * HD] = jnp.ones((BLOCK, HD), jnp.bfloat16)

    def fresh_scores(rows, c):
        token = lax.broadcasted_iota(jnp.int32, (TILE * QR, HD), 0) // GROUP
        seen = key_pos <= words[c, INDEX] * TOK + token
        return jnp.where(seen, scores_of(qa[rows, :], na[...]), FAR)

    def exact(rows, c):
        sums, tops = state_out
        if first:
            sums[rows, :] = jnp.zeros((TILE * QR, 2 * HD), jnp.float32)
        else:
            sums[rows, :] = state_in[0][rows, :]

        def block(scores, values):
            old = tops[rows, :]
            new = jnp.maximum(old, jnp.max(scores, axis=1, keepdims=True))
            factor = jnp.exp2((old - new) * SCALE)
            weights = jnp.exp2((scores - new) * SCALE).astype(jnp.bfloat16)
            product = jnp.dot(weights, values, preferred_element_type=jnp.float32)
            sums[rows, :] = sums[rows, :] * jnp.concatenate([factor, factor], axis=1) + product
            tops[rows, :] = new

        def slot(i, carry):
            at = pl.ds(pl.multiple_of(i * BLOCK, BLOCK), BLOCK)
            block(scores_of(qa[rows, :], ka[at, :]), va[at, :])
            return carry

        lax.fori_loop(0, sources * SLOTS, slot, 0)
        if last:
            block(fresh_scores(rows, c), nva[...])

    def chunk(i, carry):
        c = i * TILE
        rows = pl.ds(pl.multiple_of(c * QR, QR), TILE * QR)
        low, high = words[c, TOKEN_CHAT], words[c + TILE - 1, TOKEN_CHAT + TOK - 1]

        def own_scores(i):
            q = queries[c + i, 0:QR, :].astype(jnp.float32)
            k = queries[c + i, QR : QR + TOK, :].astype(jnp.float32)
            k = jnp.broadcast_to(k[:, None, :], (TOK, GROUP, HD)).reshape(QR, HD)
            return jnp.broadcast_to(jnp.sum(q * k, axis=1, keepdims=True), (QR, HD))

        sums, tops = state_out
        if first:
            tops[rows, :] = jnp.concatenate([own_scores(i) for i in range(TILE)], axis=0)
            sums[rows, :] = jnp.zeros((TILE * QR, 2 * HD), jnp.float32)
        else:
            tops[rows, :] = state_in[1][rows, :]
            sums[rows, :] = state_in[0][rows, :]

        def add(scores, values):
            shift = tops[rows, :] * SCALE
            wide = jnp.concatenate([shift] * (scores.shape[1] // HD), axis=1)
            weights = jnp.exp2(scores * SCALE - wide).astype(jnp.bfloat16)
            sums[rows, :] += jnp.dot(weights, values, preferred_element_type=jnp.float32)

        def source(s, carry):
            begin, end = jnp.int32(0), jnp.int32(0)
            for slot in range(SLOTS):
                chat = words[MEMBERS + s, CHAT + slot]
                begin += (chat < low).astype(jnp.int32)
                end += (chat <= high).astype(jnp.int32)
            count = end - begin

            def some(slots):
                start = s * SLOTS + jnp.minimum(begin, SLOTS - slots)
                at = pl.ds(pl.multiple_of(start * BLOCK, BLOCK), slots * BLOCK)
                add(scores_of(qa[rows, :], ka[at, :]), va[at, :])

            under = 0
            for slots in WIDTHS:
                pl.when((count > under) & (count <= slots))(functools.partial(some, slots))
                under = slots
            return carry

        lax.fori_loop(0, sources, source, 0)
        if last:
            add(fresh_scores(rows, c), nva[...])
        fine = jnp.max(sums[rows, HD : 2 * HD]) < HIGHEST

        @pl.when(jnp.logical_not(fine))
        def _():
            exact(rows, c)

        return carry

    lax.fori_loop(0, MEMBERS // TILE, chunk, 0)

    if last:
        row = lax.broadcasted_iota(jnp.int32, (16, HD), 0)

        def close(c, carry):
            rows = pl.ds(pl.multiple_of(c * QR, QR), QR)
            sums = state_out[0][rows, :]
            total = jnp.maximum(sums[:, HD : 2 * HD], LOWEST)
            normal = (sums[:, 0:HD] / total).astype(jnp.bfloat16)
            logs = (state_out[1][rows, :] * SCALE + jnp.log2(total)).T
            for j in range(HEADS):
                piece = c * HEADS + j
                out[piece, 0:PIECE, :] = normal[j * PIECE : (j + 1) * PIECE, :]
                line = logs[0:16, (j // 2) * HD : (j // 2 + 1) * HD]
                top = line.astype(jnp.bfloat16).astype(jnp.float32)
                rest = line - top
                middle = rest.astype(jnp.bfloat16).astype(jnp.float32)
                low = rest - middle
                terms = jnp.where(row == 0, top, jnp.where(row == 1, middle, low))
                out[piece, PIECE:SENT, :] = terms.astype(jnp.bfloat16)
            return carry

        lax.fori_loop(0, MEMBERS, close, 0)


def attend(queries, packs, fresh, state, last=False):
    sources, first = len(packs), state is None
    operands = [queries, *packs, *fresh]
    specs = [VMEM] * (1 + sources)
    tail = pl.BlockSpec((pl.Element(3 * TOK), pl.Element(HD)), lambda i: (FRESH_K, 0))
    specs += [tail] * len(fresh)
    if not first:
        operands += state
        specs += [VMEM, VMEM]
    rows = MEMBERS * QR
    state_shapes = [(rows, 2 * HD), (rows, HD)]
    if last:
        out_shape = jax.ShapeDtypeStruct((MEMBERS * HEADS, SENT, HD), jnp.bfloat16)
    else:
        out_shape = [jax.ShapeDtypeStruct(s, jnp.float32) for s in state_shapes]
    scratch = [
        pltpu.VMEM((rows, 2 * HD), jnp.bfloat16),
        pltpu.VMEM((3 * MEMBERS, HD), jnp.int32),
        pltpu.SMEM((3 * MEMBERS, HD), jnp.int32),
        pltpu.SemaphoreType.DMA,
    ]
    scratch += [pltpu.VMEM((sources * ROWS, 2 * HD), jnp.bfloat16)] * 2
    if last:
        scratch += [pltpu.VMEM((BLOCK, 2 * HD), jnp.bfloat16)] * 2
        scratch += [pltpu.VMEM(s, jnp.float32) for s in state_shapes]
    return pl.pallas_call(
        functools.partial(attend_kernel, sources, first, last),
        grid=(1,),
        out_shape=out_shape,
        in_specs=specs,
        out_specs=VMEM if last else [VMEM] * 2,
        scratch_shapes=scratch,
        compiler_params=params(),
        cost_estimate=pl.CostEstimate(
            flops=sources * 4 * rows * ROWS * HD,
            bytes_accessed=sources * ROWS * HD * 4 + rows * HD * 18,
            transcendentals=sources * rows * ROWS,
        ),
        name="attend_last" if last else "attend",
    )(*operands)


def finish_kernel(place, parts, out, turned, held):
    top = None
    lines = []
    for z in range(MEMBERS):
        rows = []
        for h in range(HEADS):
            terms = parts[z * HEADS + h, PIECE:SENT, :].astype(jnp.float32)
            rows.append(terms[0:1, :] + terms[1:2, :] + terms[2:3, :])
        lines.append(rows)
    shares = [[None] * HEADS for _ in range(MEMBERS)]
    for h in range(HEADS):
        top = lines[0][h]
        for z in range(1, MEMBERS):
            top = jnp.maximum(top, lines[z][h])
        powers = [jnp.exp2(lines[z][h] - top) for z in range(MEMBERS)]
        whole = powers[0]
        for power in powers[1:]:
            whole = whole + power
        for z in range(MEMBERS):
            shares[z][h] = powers[z] / whole
    for z in range(MEMBERS):
        for h in range(HEADS):
            at = z * HEADS + h
            turned[at : at + 1, :] = shares[z][h]
    held[...] = turned[...].T
    at = pl.multiple_of(lax.rem(place[1], 2) * PIECE, PIECE)
    columns = held[pl.ds(at, PIECE), :]
    for h in range(HEADS):
        total = None
        for z in range(MEMBERS):
            i = z * HEADS + h
            term = parts[i, 0:PIECE, :].astype(jnp.float32) * columns[:, i : i + 1]
            total = term if total is None else total + term
        turned[0:PIECE, :] = total
        for g in range(GROUP):
            at = (h * GROUP + g) * HD
            out[:, at : at + HD] = turned[pl.ds(g, TOK // HEADS, stride=GROUP), :].astype(jnp.bfloat16)


def finish(place, parts):
    return pl.pallas_call(
        finish_kernel,
        out_shape=jax.ShapeDtypeStruct((TOK // HEADS, HEADS * GROUP * HD), jnp.bfloat16),
        in_specs=[SMEM, VMEM],
        out_specs=VMEM,
        scratch_shapes=[pltpu.VMEM((HD, HD), jnp.float32)] * 2,
        compiler_params=params(),
        name="finish",
    )(place, parts)


YX = ("y", "xh")
HEAD = ("xl", "core")


def up(x):
    return lax.ppermute(x, "y", [(i, (i + 1) % 4) for i in range(4)])


def down(x):
    return lax.ppermute(x, "y", [(i, (i - 1) % 4) for i in range(4)])


def across(x):
    return lax.ppermute(x, "xh", [(0, 1), (1, 0)])


def per_device(queries, cache_keys, cache_values, new_keys, new_values, block_chat, block_fill, new_chat):
    place = jnp.stack([lax.axis_index(("y", "xh", "z")), lax.axis_index(HEAD)]).astype(jnp.int32)
    mine, many = prepare(
        place,
        block_chat,
        block_fill,
        new_chat,
        queries.reshape(QR, HD),
        cache_keys[:, 0, :],
        cache_values[:, 0, :],
        new_keys[:, 0, :],
        new_values[:, 0, :],
    )
    before, after, beside = up(mine), down(mine), across(mine)
    shared = lax.all_to_all(many, "z", split_axis=0, concat_axis=0, tiled=True)
    beside_before, opposite, beside_after = up(beside), down(after), across(after)
    far = across(opposite)
    near = [mine, after, beside, before, opposite]
    state = attend(shared, near, [], None)
    fresh = [mine, before, after, beside, beside_before, opposite, beside_after, far]
    parts = attend(shared, [beside_before, beside_after, far], fresh, state, last=True)
    parts = lax.all_to_all(parts, ("z",) + HEAD, split_axis=0, concat_axis=0, tiled=True)
    return finish(place, parts)


def solution(mesh):
    fine = Mesh(mesh.devices.reshape(4, 2, 8, 2, 2), ("y", "xh", "z", "xl", "core"))
    ctx = ("y", "xh", "z")
    rows = P(ctx, HEAD, None)
    return jax.shard_map(
        per_device,
        mesh=fine,
        in_specs=(rows,) * 5 + (P(ctx),) * 3,
        out_specs=P(ctx + HEAD, None),
        check_vma=False,
    )
```

```python
import functools
import math

import jax
import jax.numpy as jnp
from jax import lax
from jax.experimental import pallas as pl
from jax.experimental.pallas import tpu as pltpu
from jax.sharding import Mesh, PartitionSpec as P

BLOCK = 128
SLOTS = 8
ROWS = SLOTS * BLOCK
TOK = 16
GROUP = 16
HD = 128
QR = TOK * GROUP
MEMBERS = 8
HEADS = 4
FAR = -1e30
SCALE = HD**-0.5 * math.log2(math.e)
VMEM = pl.BlockSpec(memory_space=pltpu.VMEM)
SMEM = pl.BlockSpec(memory_space=pltpu.SMEM)
ANY = pl.BlockSpec(memory_space=pl.ANY)
VALUES = ROWS
FRESH_K = 2 * ROWS
FRESH_V = FRESH_K + TOK
DESC = FRESH_V + TOK
PACK = DESC + TOK
SHARED = QR + 2 * TOK
CHAT, FILL, TOKEN_CHAT, INDEX = 0, 8, 16, 32
PIECE = QR // HEADS
SENT = PIECE + 16
WIDTHS = (2, 3, 4, 6, 8)
TILE = 4
HIGHEST = 2.0**80
LOWEST = 2.0**-120


def params():
    return pltpu.CompilerParams(vmem_limit_bytes=36 * 1024 * 1024)


def prepare_kernel(bc, bf, nc, q, k, v, nk, nv, pack, many, sems):
    copies = [
        (k, pack.at[pl.ds(0, ROWS)]),
        (v, pack.at[pl.ds(VALUES, ROWS)]),
        (nk, pack.at[pl.ds(FRESH_K, TOK)]),
        (nv, pack.at[pl.ds(FRESH_V, TOK)]),
        (q, many.at[0, pl.ds(0, QR)]),
    ]
    started = []
    for i, (src, dst) in enumerate(copies):
        copy = pltpu.make_async_copy(src, dst, sems.at[i])
        copy.start()
        started.append(copy)
    lane = lax.broadcasted_iota(jnp.int32, (TOK, HD), 1)
    row = jnp.where(lane == INDEX, lax.axis_index(("y", "xh", "z")), 0)
    for i in range(SLOTS):
        row = jnp.where(lane == CHAT + i, bc[i], row)
        row = jnp.where(lane == FILL + i, bf[i], row)
    for i in range(TOK):
        row = jnp.where(lane == TOKEN_CHAT + i, nc[i], row)
    desc = row.astype(jnp.float32).astype(jnp.bfloat16)
    pack[DESC:PACK, :] = desc
    for copy in started:
        copy.wait()
    own = pack[FRESH_K : FRESH_K + TOK, :]
    for i in range(MEMBERS):
        if i > 0:
            many[i, 0:QR, :] = many[0, 0:QR, :]
        many[i, QR : QR + TOK, :] = own
        many[i, QR + TOK : SHARED, :] = desc


def prepare(bc, bf, nc, q, k, v, nk, nv):
    return pl.pallas_call(
        prepare_kernel,
        out_shape=[
            jax.ShapeDtypeStruct((PACK, HD), jnp.bfloat16),
            jax.ShapeDtypeStruct((MEMBERS, SHARED, HD), jnp.bfloat16),
        ],
        in_specs=[SMEM] * 3 + [ANY] * 5,
        out_specs=[VMEM] * 2,
        scratch_shapes=[pltpu.SemaphoreType.DMA((5,))],
        compiler_params=pltpu.CompilerParams(vmem_limit_bytes=58 * 1024 * 1024),
        name="prepare",
    )(bc, bf, nc, q, k, v, nk, nv)


def scores_of(q, keys):
    return lax.dot_general(q, keys, (((1,), (1,)), ((), ())), preferred_element_type=jnp.float32)


def attend_kernel(sources, first, last, *refs):
    refs = list(refs)
    take = lambda n: [refs.pop(0) for _ in range(n)]
    queries = take(1)[0]
    packs = take(sources)
    fresh = take(MEMBERS) if last else []
    state_in = None if first else tuple(take(2))
    out = take(1)[0] if last else None
    state_out = None if last else tuple(take(2))
    qa, rows_of, words, sem = take(4)
    ka, va = take(2)
    if last:
        na, nva, sums_last, tops_last = take(4)
        state_out = (sums_last, tops_last)

    def word_row(i, tile):
        rows_of[i : i + 1, :] = tile.astype(jnp.float32).astype(jnp.int32)[0:1, :]

    for i in range(MEMBERS):
        word_row(i, queries[i, QR + TOK : SHARED, :])
    for s in range(sources):
        word_row(MEMBERS + s, packs[s][DESC:PACK, :])
    if last:
        for i in range(MEMBERS):
            word_row(2 * MEMBERS + i, fresh[i][2 * TOK : 3 * TOK, :])
    copy = pltpu.make_async_copy(rows_of, words, sem)
    copy.start()

    for s in range(sources):
        ka[s * ROWS : (s + 1) * ROWS, 0:HD] = packs[s][0:ROWS, :]
        va[s * ROWS : (s + 1) * ROWS, 0:HD] = packs[s][VALUES : VALUES + ROWS, :]
    va[:, HD : 2 * HD] = jnp.ones((sources * ROWS, HD), jnp.bfloat16)
    copy.wait()

    lane = lax.broadcasted_iota(jnp.int32, (TOK, HD), 1)
    for i in range(MEMBERS):
        qa[i * QR : (i + 1) * QR, 0:HD] = queries[i, 0:QR, :]
        for t in range(TOK):
            rows = slice(i * QR + t * GROUP, i * QR + (t + 1) * GROUP)
            hot = jnp.where(lane == words[i, TOKEN_CHAT + t], 1.0, 0.0)
            qa[rows, HD : 2 * HD] = hot.astype(jnp.bfloat16)
    lane = lax.broadcasted_iota(jnp.int32, (BLOCK, HD), 1)
    row = lax.broadcasted_iota(jnp.int32, (BLOCK, HD), 0)
    for s in range(sources):
        for slot in range(SLOTS):
            live = (lane == words[MEMBERS + s, CHAT + slot]) & (row < words[MEMBERS + s, FILL + slot])
            at = slice(s * ROWS + slot * BLOCK, s * ROWS + (slot + 1) * BLOCK)
            ka[at, HD : 2 * HD] = jnp.where(live, 0.0, FAR).astype(jnp.bfloat16)
    if last:
        lane = lax.broadcasted_iota(jnp.int32, (TOK, HD), 1)
        row = lax.broadcasted_iota(jnp.int32, (TOK, HD), 0)
        key_lane = lax.broadcasted_iota(jnp.int32, (1, HD), 1)
        key_pos = jnp.zeros((1, HD), jnp.int32)
        for i in range(MEMBERS):
            at = slice(i * TOK, (i + 1) * TOK)
            na[at, 0:HD] = fresh[i][0:TOK, :]
            nva[at, 0:HD] = fresh[i][TOK : 2 * TOK, :]
            chat = jnp.zeros((TOK, HD), jnp.int32)
            for t in range(TOK):
                chat = jnp.where(row == t, words[2 * MEMBERS + i, TOKEN_CHAT + t], chat)
            na[at, HD : 2 * HD] = jnp.where(lane == chat, 0.0, FAR).astype(jnp.bfloat16)
            start = words[2 * MEMBERS + i, INDEX] * TOK
            key_pos = jnp.where(key_lane // TOK == i, start + key_lane % TOK, key_pos)
        nva[:, HD : 2 * HD] = jnp.ones((BLOCK, HD), jnp.bfloat16)

    def fresh_scores(rows, c):
        token = lax.broadcasted_iota(jnp.int32, (TILE * QR, HD), 0) // GROUP
        seen = key_pos <= words[c, INDEX] * TOK + token
        return jnp.where(seen, scores_of(qa[rows, :], na[...]), FAR)

    def exact(rows, c):
        sums, tops = state_out
        if first:
            sums[rows, :] = jnp.zeros((TILE * QR, 2 * HD), jnp.float32)
        else:
            sums[rows, :] = state_in[0][rows, :]

        def block(scores, values):
            old = tops[rows, :]
            new = jnp.maximum(old, jnp.max(scores, axis=1, keepdims=True))
            factor = jnp.exp2((old - new) * SCALE)
            weights = jnp.exp2((scores - new) * SCALE).astype(jnp.bfloat16)
            product = jnp.dot(weights, values, preferred_element_type=jnp.float32)
            sums[rows, :] = sums[rows, :] * jnp.concatenate([factor, factor], axis=1) + product
            tops[rows, :] = new

        def slot(i, carry):
            at = pl.ds(pl.multiple_of(i * BLOCK, BLOCK), BLOCK)
            block(scores_of(qa[rows, :], ka[at, :]), va[at, :])
            return carry

        lax.fori_loop(0, sources * SLOTS, slot, 0)
        if last:
            block(fresh_scores(rows, c), nva[...])

    def chunk(i, carry):
        c = i * TILE
        rows = pl.ds(pl.multiple_of(c * QR, QR), TILE * QR)
        low, high = words[c, TOKEN_CHAT], words[c + TILE - 1, TOKEN_CHAT + TOK - 1]

        def own_scores(i):
            q = queries[c + i, 0:QR, :].astype(jnp.float32)
            k = queries[c + i, QR : QR + TOK, :].astype(jnp.float32)
            k = jnp.broadcast_to(k[:, None, :], (TOK, GROUP, HD)).reshape(QR, HD)
            return jnp.broadcast_to(jnp.sum(q * k, axis=1, keepdims=True), (QR, HD))

        sums, tops = state_out
        if first:
            tops[rows, :] = jnp.concatenate([own_scores(i) for i in range(TILE)], axis=0)
            sums[rows, :] = jnp.zeros((TILE * QR, 2 * HD), jnp.float32)
        else:
            tops[rows, :] = state_in[1][rows, :]
            sums[rows, :] = state_in[0][rows, :]

        def add(scores, values):
            shift = tops[rows, :] * SCALE
            wide = jnp.concatenate([shift] * (scores.shape[1] // HD), axis=1)
            weights = jnp.exp2(scores * SCALE - wide).astype(jnp.bfloat16)
            sums[rows, :] += jnp.dot(weights, values, preferred_element_type=jnp.float32)

        def source(s, carry):
            begin, end = jnp.int32(0), jnp.int32(0)
            for slot in range(SLOTS):
                chat = words[MEMBERS + s, CHAT + slot]
                begin += (chat < low).astype(jnp.int32)
                end += (chat <= high).astype(jnp.int32)
            count = end - begin

            def some(slots):
                start = s * SLOTS + jnp.minimum(begin, SLOTS - slots)
                at = pl.ds(pl.multiple_of(start * BLOCK, BLOCK), slots * BLOCK)
                add(scores_of(qa[rows, :], ka[at, :]), va[at, :])

            under = 0
            for slots in WIDTHS:
                pl.when((count > under) & (count <= slots))(functools.partial(some, slots))
                under = slots
            return carry

        lax.fori_loop(0, sources, source, 0)
        if last:
            add(fresh_scores(rows, c), nva[...])
        fine = jnp.max(sums[rows, HD : 2 * HD]) < HIGHEST

        @pl.when(jnp.logical_not(fine))
        def _():
            exact(rows, c)

        return carry

    lax.fori_loop(0, MEMBERS // TILE, chunk, 0)

    if last:
        row = lax.broadcasted_iota(jnp.int32, (16, HD), 0)

        def close(c, carry):
            rows = pl.ds(pl.multiple_of(c * QR, QR), QR)
            sums = state_out[0][rows, :]
            total = jnp.maximum(sums[:, HD : 2 * HD], LOWEST)
            normal = (sums[:, 0:HD] / total).astype(jnp.bfloat16)
            logs = (state_out[1][rows, :] * SCALE + jnp.log2(total)).T
            for j in range(HEADS):
                piece = c * HEADS + j
                out[piece, 0:PIECE, :] = normal[j * PIECE : (j + 1) * PIECE, :]
                line = logs[0:16, (j // 2) * HD : (j // 2 + 1) * HD]
                top = line.astype(jnp.bfloat16).astype(jnp.float32)
                rest = line - top
                middle = rest.astype(jnp.bfloat16).astype(jnp.float32)
                low = rest - middle
                terms = jnp.where(row == 0, top, jnp.where(row == 1, middle, low))
                out[piece, PIECE:SENT, :] = terms.astype(jnp.bfloat16)
            return carry

        lax.fori_loop(0, MEMBERS, close, 0)


def attend(queries, packs, fresh, state, last=False):
    sources, first = len(packs), state is None
    operands = [queries, *packs, *fresh]
    specs = [VMEM] * (1 + sources)
    tail = pl.BlockSpec((pl.Element(3 * TOK), pl.Element(HD)), lambda i: (FRESH_K, 0))
    specs += [tail] * len(fresh)
    if not first:
        operands += state
        specs += [VMEM, VMEM]
    rows = MEMBERS * QR
    state_shapes = [(rows, 2 * HD), (rows, HD)]
    if last:
        out_shape = jax.ShapeDtypeStruct((MEMBERS * HEADS, SENT, HD), jnp.bfloat16)
    else:
        out_shape = [jax.ShapeDtypeStruct(s, jnp.float32) for s in state_shapes]
    scratch = [
        pltpu.VMEM((rows, 2 * HD), jnp.bfloat16),
        pltpu.VMEM((3 * MEMBERS, HD), jnp.int32),
        pltpu.SMEM((3 * MEMBERS, HD), jnp.int32),
        pltpu.SemaphoreType.DMA,
    ]
    scratch += [pltpu.VMEM((sources * ROWS, 2 * HD), jnp.bfloat16)] * 2
    if last:
        scratch += [pltpu.VMEM((BLOCK, 2 * HD), jnp.bfloat16)] * 2
        scratch += [pltpu.VMEM(s, jnp.float32) for s in state_shapes]
    return pl.pallas_call(
        functools.partial(attend_kernel, sources, first, last),
        grid=(1,),
        out_shape=out_shape,
        in_specs=specs,
        out_specs=VMEM if last else [VMEM] * 2,
        scratch_shapes=scratch,
        compiler_params=params(),
        cost_estimate=pl.CostEstimate(
            flops=sources * 4 * rows * ROWS * HD,
            bytes_accessed=sources * ROWS * HD * 4 + rows * HD * 18,
            transcendentals=sources * rows * ROWS,
        ),
        name="attend_last" if last else "attend",
    )(*operands)


def finish_kernel(parts, out, turned, held):
    top = None
    lines = []
    for z in range(MEMBERS):
        rows = []
        for h in range(HEADS):
            terms = parts[z * HEADS + h, PIECE:SENT, :].astype(jnp.float32)
            rows.append(terms[0:1, :] + terms[1:2, :] + terms[2:3, :])
        lines.append(rows)
    shares = [[None] * HEADS for _ in range(MEMBERS)]
    for h in range(HEADS):
        top = lines[0][h]
        for z in range(1, MEMBERS):
            top = jnp.maximum(top, lines[z][h])
        powers = [jnp.exp2(lines[z][h] - top) for z in range(MEMBERS)]
        whole = powers[0]
        for power in powers[1:]:
            whole = whole + power
        for z in range(MEMBERS):
            shares[z][h] = powers[z] / whole
    for z in range(MEMBERS):
        for h in range(HEADS):
            at = z * HEADS + h
            turned[at : at + 1, :] = shares[z][h]
    held[...] = turned[...].T
    at = pl.multiple_of(lax.axis_index("core") * PIECE, PIECE)
    columns = held[pl.ds(at, PIECE), :]
    for h in range(HEADS):
        total = None
        for z in range(MEMBERS):
            i = z * HEADS + h
            term = parts[i, 0:PIECE, :].astype(jnp.float32) * columns[:, i : i + 1]
            total = term if total is None else total + term
        turned[0:PIECE, :] = total
        for g in range(GROUP):
            at = (h * GROUP + g) * HD
            out[:, at : at + HD] = turned[pl.ds(g, TOK // HEADS, stride=GROUP), :].astype(jnp.bfloat16)


def finish(parts):
    return pl.pallas_call(
        finish_kernel,
        out_shape=jax.ShapeDtypeStruct((TOK // HEADS, HEADS * GROUP * HD), jnp.bfloat16),
        in_specs=[VMEM],
        out_specs=VMEM,
        scratch_shapes=[pltpu.VMEM((HD, HD), jnp.float32)] * 2,
        compiler_params=params(),
        name="finish",
    )(parts)


YX = ("y", "xh")
HEAD = ("xl", "core")


def up(x):
    return lax.ppermute(x, "y", [(i, (i + 1) % 4) for i in range(4)])


def down(x):
    return lax.ppermute(x, "y", [(i, (i - 1) % 4) for i in range(4)])


def across(x):
    return lax.ppermute(x, "xh", [(0, 1), (1, 0)])


def per_device(queries, cache_keys, cache_values, new_keys, new_values, block_chat, block_fill, new_chat):
    mine, many = prepare(
        block_chat,
        block_fill,
        new_chat,
        queries.reshape(QR, HD),
        cache_keys[:, 0, :],
        cache_values[:, 0, :],
        new_keys[:, 0, :],
        new_values[:, 0, :],
    )
    before, after, beside = up(mine), down(mine), across(mine)
    shared = lax.all_to_all(many, "z", split_axis=0, concat_axis=0, tiled=True)
    beside_before, opposite, beside_after = up(beside), down(after), across(after)
    far = across(opposite)
    near = [mine, after, beside, before, opposite]
    state = attend(shared, near, [], None)
    fresh = [mine, before, after, beside, beside_before, opposite, beside_after, far]
    parts = attend(shared, [beside_before, beside_after, far], fresh, state, last=True)
    parts = lax.all_to_all(parts, ("z",) + HEAD, split_axis=0, concat_axis=0, tiled=True)
    return finish(parts)


def solution(mesh):
    fine = Mesh(mesh.devices.reshape(4, 2, 8, 2, 2), ("y", "xh", "z", "xl", "core"))
    ctx = ("y", "xh", "z")
    rows = P(ctx, HEAD, None)
    return jax.shard_map(
        per_device,
        mesh=fine,
        in_specs=(rows,) * 5 + (P(ctx),) * 3,
        out_specs=P(ctx + HEAD, None),
        check_vma=False,
    )
```

```python
import functools
import math

import jax
import jax.numpy as jnp
from jax import lax
from jax.experimental import pallas as pl
from jax.experimental.pallas import tpu as pltpu
from jax.sharding import Mesh, PartitionSpec as P

BLOCK = 128
SLOTS = 8
ROWS = SLOTS * BLOCK
TOK = 16
GROUP = 16
HD = 128
QR = TOK * GROUP
MEMBERS = 8
HEADS = 4
FAR = -1e30
SCALE = HD**-0.5 * math.log2(math.e)
VMEM = pl.BlockSpec(memory_space=pltpu.VMEM)
SMEM = pl.BlockSpec(memory_space=pltpu.SMEM)
ANY = pl.BlockSpec(memory_space=pl.ANY)
VALUES = ROWS
FRESH_K = 2 * ROWS
FRESH_V = FRESH_K + TOK
DESC = FRESH_V + TOK
PACK = DESC + TOK
SHARED = QR + 2 * TOK
CHAT, FILL, TOKEN_CHAT, INDEX = 0, 8, 16, 32
PIECE = QR // HEADS
SENT = PIECE + 16
WIDTHS = (2, 3, 4, 6, 8)
TILE = 4
HIGHEST = 2.0**80
LOWEST = 2.0**-120


def params():
    return pltpu.CompilerParams(vmem_limit_bytes=36 * 1024 * 1024)


def prepare_kernel(bc, bf, nc, q, k, v, nk, nv, pack, many, sems):
    copies = [
        (k, pack.at[pl.ds(0, ROWS)]),
        (v, pack.at[pl.ds(VALUES, ROWS)]),
        (nk, pack.at[pl.ds(FRESH_K, TOK)]),
        (nv, pack.at[pl.ds(FRESH_V, TOK)]),
        (q, many.at[0, pl.ds(0, QR)]),
    ]
    started = []
    for i, (src, dst) in enumerate(copies):
        copy = pltpu.make_async_copy(src, dst, sems.at[i])
        copy.start()
        started.append(copy)
    lane = lax.broadcasted_iota(jnp.int32, (TOK, HD), 1)
    row = jnp.where(lane == INDEX, lax.axis_index(("y", "xh", "z")), 0)
    for i in range(SLOTS):
        row = jnp.where(lane == CHAT + i, bc[i], row)
        row = jnp.where(lane == FILL + i, bf[i], row)
    for i in range(TOK):
        row = jnp.where(lane == TOKEN_CHAT + i, nc[i], row)
    desc = row.astype(jnp.float32).astype(jnp.bfloat16)
    pack[DESC:PACK, :] = desc
    for copy in started:
        copy.wait()
    own = pack[FRESH_K : FRESH_K + TOK, :]
    for i in range(MEMBERS):
        if i > 0:
            many[i, 0:QR, :] = many[0, 0:QR, :]
        many[i, QR : QR + TOK, :] = own
        many[i, QR + TOK : SHARED, :] = desc


def prepare(bc, bf, nc, q, k, v, nk, nv):
    return pl.pallas_call(
        prepare_kernel,
        out_shape=[
            jax.ShapeDtypeStruct((PACK, HD), jnp.bfloat16),
            jax.ShapeDtypeStruct((MEMBERS, SHARED, HD), jnp.bfloat16),
        ],
        in_specs=[SMEM] * 3 + [ANY] * 5,
        out_specs=[VMEM] * 2,
        scratch_shapes=[pltpu.SemaphoreType.DMA((5,))],
        compiler_params=pltpu.CompilerParams(vmem_limit_bytes=58 * 1024 * 1024),
        name="prepare",
    )(bc, bf, nc, q, k, v, nk, nv)


def scores_of(q, keys):
    return lax.dot_general(q, keys, (((1,), (1,)), ((), ())), preferred_element_type=jnp.float32)


def attend_kernel(sources, first, last, *refs):
    refs = list(refs)
    take = lambda n: [refs.pop(0) for _ in range(n)]
    queries = take(1)[0]
    packs = take(sources)
    fresh = take(MEMBERS) if last else []
    state_in = None if first else tuple(take(2))
    out = take(1)[0] if last else None
    state_out = None if last else tuple(take(2))
    qa, rows_of, words, sem = take(4)
    ka, va = take(2)
    if last:
        na, nva, sums_last, tops_last = take(4)
        state_out = (sums_last, tops_last)

    def word_row(i, tile):
        rows_of[i : i + 1, :] = tile.astype(jnp.float32).astype(jnp.int32)[0:1, :]

    for i in range(MEMBERS):
        word_row(i, queries[i, QR + TOK : SHARED, :])
    for s in range(sources):
        word_row(MEMBERS + s, packs[s][DESC:PACK, :])
    if last:
        for i in range(MEMBERS):
            word_row(2 * MEMBERS + i, fresh[i][2 * TOK : 3 * TOK, :])
    copy = pltpu.make_async_copy(rows_of, words, sem)
    copy.start()

    for s in range(sources):
        ka[s * ROWS : (s + 1) * ROWS, 0:HD] = packs[s][0:ROWS, :]
        va[s * ROWS : (s + 1) * ROWS, 0:HD] = packs[s][VALUES : VALUES + ROWS, :]
    va[:, HD : 2 * HD] = jnp.ones((sources * ROWS, HD), jnp.bfloat16)
    copy.wait()

    lane = lax.broadcasted_iota(jnp.int32, (TOK, HD), 1)
    for i in range(MEMBERS):
        qa[i * QR : (i + 1) * QR, 0:HD] = queries[i, 0:QR, :]
        for t in range(TOK):
            rows = slice(i * QR + t * GROUP, i * QR + (t + 1) * GROUP)
            hot = jnp.where(lane == words[i, TOKEN_CHAT + t], 1.0, 0.0)
            qa[rows, HD : 2 * HD] = hot.astype(jnp.bfloat16)
    lane = lax.broadcasted_iota(jnp.int32, (BLOCK, HD), 1)
    row = lax.broadcasted_iota(jnp.int32, (BLOCK, HD), 0)
    for s in range(sources):
        for slot in range(SLOTS):
            live = (lane == words[MEMBERS + s, CHAT + slot]) & (row < words[MEMBERS + s, FILL + slot])
            at = slice(s * ROWS + slot * BLOCK, s * ROWS + (slot + 1) * BLOCK)
            ka[at, HD : 2 * HD] = jnp.where(live, 0.0, FAR).astype(jnp.bfloat16)
    if last:
        lane = lax.broadcasted_iota(jnp.int32, (TOK, HD), 1)
        row = lax.broadcasted_iota(jnp.int32, (TOK, HD), 0)
        key_lane = lax.broadcasted_iota(jnp.int32, (1, HD), 1)
        key_pos = jnp.zeros((1, HD), jnp.int32)
        for i in range(MEMBERS):
            at = slice(i * TOK, (i + 1) * TOK)
            na[at, 0:HD] = fresh[i][0:TOK, :]
            nva[at, 0:HD] = fresh[i][TOK : 2 * TOK, :]
            chat = jnp.zeros((TOK, HD), jnp.int32)
            for t in range(TOK):
                chat = jnp.where(row == t, words[2 * MEMBERS + i, TOKEN_CHAT + t], chat)
            na[at, HD : 2 * HD] = jnp.where(lane == chat, 0.0, FAR).astype(jnp.bfloat16)
            start = words[2 * MEMBERS + i, INDEX] * TOK
            key_pos = jnp.where(key_lane // TOK == i, start + key_lane % TOK, key_pos)
        nva[:, HD : 2 * HD] = jnp.ones((BLOCK, HD), jnp.bfloat16)

    def fresh_scores(rows, c):
        token = lax.broadcasted_iota(jnp.int32, (TILE * QR, HD), 0) // GROUP
        seen = key_pos <= words[c, INDEX] * TOK + token
        return jnp.where(seen, scores_of(qa[rows, :], na[...]), FAR)

    def exact(rows, c):
        sums, tops = state_out
        if first:
            sums[rows, :] = jnp.zeros((TILE * QR, 2 * HD), jnp.float32)
        else:
            sums[rows, :] = state_in[0][rows, :]

        def block(scores, values):
            old = tops[rows, :]
            new = jnp.maximum(old, jnp.max(scores, axis=1, keepdims=True))
            factor = jnp.exp2((old - new) * SCALE)
            weights = jnp.exp2((scores - new) * SCALE).astype(jnp.bfloat16)
            product = jnp.dot(weights, values, preferred_element_type=jnp.float32)
            sums[rows, :] = sums[rows, :] * jnp.concatenate([factor, factor], axis=1) + product
            tops[rows, :] = new

        def slot(i, carry):
            at = pl.ds(pl.multiple_of(i * BLOCK, BLOCK), BLOCK)
            block(scores_of(qa[rows, :], ka[at, :]), va[at, :])
            return carry

        lax.fori_loop(0, sources * SLOTS, slot, 0)
        if last:
            block(fresh_scores(rows, c), nva[...])

    def chunk(i, carry):
        c = i * TILE
        rows = pl.ds(pl.multiple_of(c * QR, QR), TILE * QR)
        low, high = words[c, TOKEN_CHAT], words[c + TILE - 1, TOKEN_CHAT + TOK - 1]

        def own_scores(i):
            q = queries[c + i, 0:QR, :].astype(jnp.float32)
            k = queries[c + i, QR : QR + TOK, :].astype(jnp.float32)
            k = jnp.broadcast_to(k[:, None, :], (TOK, GROUP, HD)).reshape(QR, HD)
            return jnp.broadcast_to(jnp.sum(q * k, axis=1, keepdims=True), (QR, HD))

        sums, tops = state_out
        if first:
            tops[rows, :] = jnp.concatenate([own_scores(i) for i in range(TILE)], axis=0)
            sums[rows, :] = jnp.zeros((TILE * QR, 2 * HD), jnp.float32)
        else:
            tops[rows, :] = state_in[1][rows, :]
            sums[rows, :] = state_in[0][rows, :]

        def add(scores, values):
            shift = tops[rows, :] * SCALE
            wide = jnp.concatenate([shift] * (scores.shape[1] // HD), axis=1)
            weights = jnp.exp2(scores * SCALE - wide).astype(jnp.bfloat16)
            sums[rows, :] += jnp.dot(weights, values, preferred_element_type=jnp.float32)

        def source(s, carry):
            begin, end = jnp.int32(0), jnp.int32(0)
            for slot in range(SLOTS):
                chat = words[MEMBERS + s, CHAT + slot]
                begin += (chat < low).astype(jnp.int32)
                end += (chat <= high).astype(jnp.int32)
            count = end - begin

            def some(slots):
                start = s * SLOTS + jnp.minimum(begin, SLOTS - slots)
                at = pl.ds(pl.multiple_of(start * BLOCK, BLOCK), slots * BLOCK)
                add(scores_of(qa[rows, :], ka[at, :]), va[at, :])

            under = 0
            for slots in WIDTHS:
                pl.when((count > under) & (count <= slots))(functools.partial(some, slots))
                under = slots
            return carry

        lax.fori_loop(0, sources, source, 0)
        if last:
            add(fresh_scores(rows, c), nva[...])
        fine = jnp.max(sums[rows, HD : 2 * HD]) < HIGHEST

        @pl.when(jnp.logical_not(fine))
        def _():
            exact(rows, c)

        return carry

    lax.fori_loop(0, MEMBERS // TILE, chunk, 0)

    if last:
        row = lax.broadcasted_iota(jnp.int32, (16, HD), 0)

        def close(c, carry):
            rows = pl.ds(pl.multiple_of(c * QR, QR), QR)
            sums = state_out[0][rows, :]
            total = jnp.maximum(sums[:, HD : 2 * HD], LOWEST)
            normal = (sums[:, 0:HD] / total).astype(jnp.bfloat16)
            logs = (state_out[1][rows, :] * SCALE + jnp.log2(total)).T
            for j in range(HEADS):
                piece = c * HEADS + j
                out[piece, 0:PIECE, :] = normal[j * PIECE : (j + 1) * PIECE, :]
                line = logs[0:16, (j // 2) * HD : (j // 2 + 1) * HD]
                top = line.astype(jnp.bfloat16).astype(jnp.float32)
                rest = line - top
                middle = rest.astype(jnp.bfloat16).astype(jnp.float32)
                low = rest - middle
                terms = jnp.where(row == 0, top, jnp.where(row == 1, middle, low))
                out[piece, PIECE:SENT, :] = terms.astype(jnp.bfloat16)
            return carry

        lax.fori_loop(0, MEMBERS, close, 0)


def attend(queries, packs, fresh, state, last=False):
    sources, first = len(packs), state is None
    operands = [queries, *packs, *fresh]
    specs = [VMEM] * (1 + sources)
    tail = pl.BlockSpec((pl.Element(3 * TOK), pl.Element(HD)), lambda i: (FRESH_K, 0))
    specs += [tail] * len(fresh)
    if not first:
        operands += state
        specs += [VMEM, VMEM]
    rows = MEMBERS * QR
    state_shapes = [(rows, 2 * HD), (rows, HD)]
    if last:
        out_shape = jax.ShapeDtypeStruct((MEMBERS * HEADS, SENT, HD), jnp.bfloat16)
    else:
        out_shape = [jax.ShapeDtypeStruct(s, jnp.float32) for s in state_shapes]
    scratch = [
        pltpu.VMEM((rows, 2 * HD), jnp.bfloat16),
        pltpu.VMEM((3 * MEMBERS, HD), jnp.int32),
        pltpu.SMEM((3 * MEMBERS, HD), jnp.int32),
        pltpu.SemaphoreType.DMA,
    ]
    scratch += [pltpu.VMEM((sources * ROWS, 2 * HD), jnp.bfloat16)] * 2
    if last:
        scratch += [pltpu.VMEM((BLOCK, 2 * HD), jnp.bfloat16)] * 2
        scratch += [pltpu.VMEM(s, jnp.float32) for s in state_shapes]
    return pl.pallas_call(
        functools.partial(attend_kernel, sources, first, last),
        grid=(1,),
        out_shape=out_shape,
        in_specs=specs,
        out_specs=VMEM if last else [VMEM] * 2,
        scratch_shapes=scratch,
        compiler_params=params(),
        cost_estimate=pl.CostEstimate(
            flops=sources * 4 * rows * ROWS * HD,
            bytes_accessed=sources * ROWS * HD * 4 + rows * HD * 18,
            transcendentals=sources * rows * ROWS,
        ),
        name="attend_last" if last else "attend",
    )(*operands)


def finish_kernel(parts, out, turned, held):
    top = None
    lines = []
    for z in range(MEMBERS):
        rows = []
        for h in range(HEADS):
            terms = parts[z * HEADS + h, PIECE:SENT, :].astype(jnp.float32)
            rows.append(terms[0:1, :] + terms[1:2, :] + terms[2:3, :])
        lines.append(rows)
    shares = [[None] * HEADS for _ in range(MEMBERS)]
    for h in range(HEADS):
        top = lines[0][h]
        for z in range(1, MEMBERS):
            top = jnp.maximum(top, lines[z][h])
        powers = [jnp.exp2(lines[z][h] - top) for z in range(MEMBERS)]
        whole = powers[0]
        for power in powers[1:]:
            whole = whole + power
        for z in range(MEMBERS):
            shares[z][h] = powers[z] / whole
    for z in range(MEMBERS):
        for h in range(HEADS):
            at = z * HEADS + h
            turned[at : at + 1, :] = shares[z][h]
    held[...] = turned[...].T
    at = pl.multiple_of(lax.axis_index("core") * PIECE, PIECE)
    columns = held[pl.ds(at, PIECE), :]
    for h in range(HEADS):
        total = None
        for z in range(MEMBERS):
            i = z * HEADS + h
            term = parts[i, 0:PIECE, :].astype(jnp.float32) * columns[:, i : i + 1]
            total = term if total is None else total + term
        turned[0:PIECE, :] = total
        for g in range(GROUP):
            at = (h * GROUP + g) * HD
            out[:, at : at + HD] = turned[pl.ds(g, TOK // HEADS, stride=GROUP), :].astype(jnp.bfloat16)


def finish(parts):
    return pl.pallas_call(
        finish_kernel,
        out_shape=jax.ShapeDtypeStruct((TOK // HEADS, HEADS * GROUP * HD), jnp.bfloat16),
        in_specs=[VMEM],
        out_specs=VMEM,
        scratch_shapes=[pltpu.VMEM((HD, HD), jnp.float32)] * 2,
        compiler_params=params(),
        name="finish",
    )(parts)


YX = ("y", "xh")
HEAD = ("xl", "core")


def up(x):
    return lax.ppermute(x, "y", [(i, (i + 1) % 4) for i in range(4)])


def down(x):
    return lax.ppermute(x, "y", [(i, (i - 1) % 4) for i in range(4)])


def across(x):
    return lax.ppermute(x, "xh", [(0, 1), (1, 0)])


def per_device(queries, cache_keys, cache_values, new_keys, new_values, block_chat, block_fill, new_chat):
    mine, many = prepare(
        block_chat,
        block_fill,
        new_chat,
        queries.reshape(QR, HD),
        cache_keys[:, 0, :],
        cache_values[:, 0, :],
        new_keys[:, 0, :],
        new_values[:, 0, :],
    )
    before, after, beside = up(mine), down(mine), across(mine)
    shared = lax.all_to_all(many, "z", split_axis=0, concat_axis=0, tiled=True)
    beside_before, opposite, beside_after = up(beside), down(after), across(after)
    far = across(opposite)
    near = [mine, after, beside, before, opposite]
    state = attend(shared, near, [], None)
    state = attend(shared, [beside_after, beside_before], [], state)
    fresh = [mine, before, after, beside, beside_before, opposite, beside_after, far]
    parts = attend(shared, [far], fresh, state, last=True)
    parts = lax.all_to_all(parts, ("z",) + HEAD, split_axis=0, concat_axis=0, tiled=True)
    return finish(parts)


def solution(mesh):
    fine = Mesh(mesh.devices.reshape(4, 2, 8, 2, 2), ("y", "xh", "z", "xl", "core"))
    ctx = ("y", "xh", "z")
    rows = P(ctx, HEAD, None)
    return jax.shard_map(
        per_device,
        mesh=fine,
        in_specs=(rows,) * 5 + (P(ctx),) * 3,
        out_specs=P(ctx + HEAD, None),
        check_vma=False,
    )
```
